32 devices in a mesh: groups: 2 (over y), tile: 4 (over z), win: 4 (over x, core).
Axes of the slice: x: 2, y: 2, z: 4, core: 2. Of those that a mesh axis runs over, the one named last changes fastest.
Arguments:
- phases: float32 [64, 4096, 512], P(('groups', 'win'), 'tile'), parts along dimension 0, may hold values from -3.140625 to 3.140625
- tile_blocks: int32 [4, 2], replicated, may hold values from 0 to 31, as said below
Outputs:
- correlations: float32 [8, 16, 16, 513], P(('groups', 'tile'), 'win'), parts along dimension 0
The draws below stay inside these ranges and needn't reach their ends.
There are 2 independent parts, one for each index of `groups`. The reference program is written for one: setup_inputs(seed, part) draws one part's arguments, and reference() takes and returns one part's arrays. A program takes and returns all parts, laid end to end along the dimension named above; an argument that names none is the same for every part. Nothing has to cross between parts.
Inputs may be any that keep to these rules, and one draw needn't show every extreme that they name: `tile_blocks`: each row names two different channel blocks, the first smaller than the second; no two rows name the same pair.
All inputs are finite; a program needn't handle non-finite values.
Results may differ from the reference program's by a relative error of at most 0.0003.
Values sent between devices are 32-bit elements; how exact they have to be, the bound alone decides.
No kernel may reach another device: no remote copies, remote signals or barrier semaphores. Data moves between devices by JAX's collectives and lax.ppermute only.
A program may use at most 256 MiB of HBM per device.

```python
import math
import jax
import jax.numpy as jnp
import numpy as np
from jax import lax

C = 512
F = 4096
BLOCK = 16
HALF = 256
WINDOWS = 32
TILES = 4
NBLOCK = 32


def draw_tile_blocks(key, part):
    key = jax.random.fold_in(key, 11)
    upper_a, upper_b = np.triu_indices(NBLOCK, 1)
    pair_a = jnp.asarray(upper_a.astype(np.int32))
    pair_b = jnp.asarray(upper_b.astype(np.int32))
    shuffled = jax.random.permutation(key, pair_a.shape[0])[:TILES]
    return jnp.stack([pair_a[shuffled], pair_b[shuffled]], axis=1).astype(jnp.int32)


def setup_inputs(seed: int = 0, part: int = 0) -> dict:
    arg_keys = jax.random.split(jax.random.key(seed), 3)
    own_keys = jax.random.split(jax.random.fold_in(arg_keys[2], part), 3)
    phases = jnp.clip(jax.random.uniform(own_keys[0], (WINDOWS, F, C), jnp.float32, -3.140625, 3.140625), -3.140625, 3.140625)
    tile_blocks = draw_tile_blocks(jax.random.fold_in(arg_keys[2], 71), part)
    return dict(phases=phases, tile_blocks=tile_blocks)


def lag_tables(bin_count, half_lags, windows):
    freq_index = jnp.arange(bin_count, dtype=jnp.int32)[:, None]
    lag_index = jnp.arange(2 * half_lags + 1, dtype=jnp.int32)[None, :] - half_lags
    phase_turns = jnp.mod(freq_index * lag_index, 2 * bin_count).astype(jnp.float32)
    angles = phase_turns * jnp.float32(math.pi / bin_count)
    weight = jnp.where(freq_index == 0, 1.0, 2.0).astype(jnp.float32) / jnp.float32(math.sqrt(2.0 * windows * bin_count))
    return (weight * jnp.cos(angles), -weight * jnp.sin(angles))

def cross_spectra(leading, trailing):
    cos_lead, sin_lead = (jnp.cos(leading), jnp.sin(leading))
    cos_trail, sin_trail = (jnp.cos(trailing), jnp.sin(trailing))
    highest = lax.Precision.HIGHEST
    cross_real = jnp.einsum('wfi,wfj->fij', cos_lead, cos_trail, precision=highest) + jnp.einsum('wfi,wfj->fij', sin_lead, sin_trail, precision=highest)
    cross_imag = jnp.einsum('wfi,wfj->fij', sin_lead, cos_trail, precision=highest) - jnp.einsum('wfi,wfj->fij', cos_lead, sin_trail, precision=highest)
    return (cross_real, cross_imag)

def to_lags(cross_real, cross_imag, cos_tab, sin_tab):
    bin_count, rows_a, rows_b = cross_real.shape
    dims = (((0,), (0,)), ((), ()))
    highest = lax.Precision.HIGHEST
    lagged = lax.dot_general(cross_real.reshape(bin_count, rows_a * rows_b), cos_tab, dims, precision=highest)
    lagged = lagged + lax.dot_general(cross_imag.reshape(bin_count, rows_a * rows_b), sin_tab, dims, precision=highest)
    return lagged.reshape(rows_a, rows_b, cos_tab.shape[1])

def reference(phases, tile_blocks):
    cos_tab, sin_tab = lag_tables(F, HALF, WINDOWS)

    def one_tile(tile_pair):
        leading = lax.dynamic_slice_in_dim(phases, (tile_pair[0] * BLOCK).astype(jnp.int32), BLOCK, 2)
        trailing = lax.dynamic_slice_in_dim(phases, (tile_pair[1] * BLOCK).astype(jnp.int32), BLOCK, 2)
        cross_real, cross_imag = cross_spectra(leading, trailing)
        return to_lags(cross_real, cross_imag, cos_tab, sin_tab)
    return lax.map(one_tile, tile_blocks)
```

```python
import functools
import math

import jax
import jax.numpy as jnp
import numpy as np
from jax import lax
from jax.experimental import pallas as pl
from jax.experimental.pallas import tpu as pltpu
from jax.sharding import PartitionSpec as P

BLOCK = 16
HALF = 256
LANES = 128
TAB_ROWS = 272
LAG_ROWS = 264
SIN_FIT = (7.0710677816e-01, -2.9462767175e-02, 3.6827228729e-04, -2.1886110623e-06, 7.1958213082e-09)
COS_FIT = (1.4142134963e+00, -1.7677635964e-01, 3.6825748950e-03, -3.0612567514e-05, 1.2790438412e-07)


def lag_tables(total_bins, bins_local, windows):
    bins = np.arange(total_bins, dtype=np.int64)
    lags = np.arange(TAB_ROWS, dtype=np.int64)
    angles = np.mod(lags[:, None] * bins[None, :], 2 * total_bins) * (math.pi / total_bins)
    weight = np.where(bins == 0, 1.0, 2.0) / math.sqrt(2.0 * windows * total_bins)
    out = []
    for values in (weight * np.cos(angles), weight * np.sin(angles)):
        values = values.astype(np.float32)
        high = values.astype(jnp.bfloat16)
        low = (values - high.astype(np.float32)).astype(jnp.bfloat16)
        out.append(np.stack([high, low]))
    table = np.stack(out)
    table = table.reshape(2, 2, TAB_ROWS, total_bins // bins_local, bins_local)
    return np.ascontiguousarray(np.moveaxis(table, 3, 0))


def horner(coefs, z):
    acc = z * coefs[-1] + coefs[-2]
    for coef in coefs[-3::-1]:
        acc = acc * z + coef
    return acc


def sin_cos(x):
    z = x * x
    t = x * horner(SIN_FIT, z)
    q = horner(COS_FIT, z)
    return t * q, 1.0 - t * t


def lag_kernel(tiles, windows, columns_ref, slice_ref, *refs):
    del columns_ref, slice_ref
    cols = 2 * tiles
    raw_refs = refs[:cols]
    idx_ref, tab_ref, keep_ref, send_ref, plane_ref, hi_re, lo_re, hi_im, lo_im, acc_ref = refs[cols:]
    step = pl.program_id(0)
    chunk = raw_refs[0].shape[1]
    per_vec = LANES // (cols * BLOCK)
    lane = lax.broadcasted_iota(jnp.int32, (LANES, LANES), 1)
    slots = [(w, m) for w in range(per_vec) for m in range(cols)]

    @pl.when(step == 0)
    def _():
        acc_ref[...] = jnp.zeros_like(acc_ref)

    for sub in range(chunk // LANES):
        rows = pl.ds(sub * LANES, LANES)
        for group in range(windows // per_vec):
            packed = None
            for slot, (w, m) in enumerate(slots):
                raw = raw_refs[m][group * per_vec + w, rows, :]
                index = jnp.broadcast_to(idx_ref[m : m + 1, :], (LANES, LANES))
                moved = jnp.take_along_axis(raw, index, axis=1)
                packed = moved if packed is None else jnp.where(lane >= slot * BLOCK, moved, packed)
            sin, cos = sin_cos(packed.T)
            both = cos + sin
            diff = cos - sin
            for slot, (w, m) in enumerate(slots):
                part = slice(slot * BLOCK, (slot + 1) * BLOCK)
                w_all = group * per_vec + w
                if m % 2 == 0:
                    three = (both[part], sin[part], cos[part])
                else:
                    three = (cos[part], diff[part], both[part])
                for p in range(3):
                    plane_ref[p, w_all, m * BLOCK : (m + 1) * BLOCK, :] = three[p]
        for tile in range(tiles):
            lead, trail = 2 * tile * BLOCK, (2 * tile + 1) * BLOCK
            for quad in range(BLOCK // 4):
                sums = [[None] * 3 for _ in range(4)]
                for w in range(windows):
                    right = [plane_ref[p, w, trail : trail + BLOCK, :] for p in range(3)]
                    for i in range(4):
                        row = lead + quad * 4 + i
                        for p in range(3):
                            left = plane_ref[p, w, row : row + 1, :]
                            prod = left * right[p]
                            sums[i][p] = prod if w == 0 else sums[i][p] + prod
                for i in range(4):
                    first = tile * BLOCK * BLOCK + (quad * 4 + i) * BLOCK
                    where = (pl.ds(first, BLOCK), pl.ds(sub * LANES, LANES))
                    real = sums[i][0] - sums[i][1]
                    imag = sums[i][0] - sums[i][2]
                    for value, hi, lo in ((real, hi_re, lo_re), (imag, hi_im, lo_im)):
                        high = value.astype(jnp.bfloat16)
                        hi[where] = high
                        lo[where] = (value - high.astype(jnp.float32)).astype(jnp.bfloat16)

    def product(table, spectra):
        return lax.dot_general(
            table, spectra, (((1,), (1,)), ((), ())), preferred_element_type=jnp.float32
        )

    pairs = BLOCK * BLOCK
    for tile in range(tiles):
        mine = pl.ds(tile * pairs, pairs)
        for part, (hi, lo) in enumerate(((hi_re, lo_re), (hi_im, lo_im))):
            tab_hi, tab_lo = tab_ref[part, 0], tab_ref[part, 1]
            total = product(tab_hi, hi[mine, :]) + product(tab_lo, hi[mine, :])
            total = total + product(tab_hi, lo[mine, :])
            acc_ref[tile, part] += total

    @pl.when(step == pl.num_programs(0) - 1)
    def _():
        half = LANES // 2
        low_lanes = lax.broadcasted_iota(jnp.int32, (LAG_ROWS, LANES), 1) < half
        for tile in range(tiles):
            for core, ref in enumerate((keep_ref, send_ref)):
                cut = (slice(0, LAG_ROWS), slice(core * LANES, (core + 1) * LANES))
                even, odd = acc_ref[(tile, 0) + cut], acc_ref[(tile, 1) + cut]
                ref[0, tile] = jnp.where(low_lanes, even, pltpu.roll(odd, half, 1))
                ref[1, tile] = jnp.where(low_lanes, pltpu.roll(even, half, 1), odd)


def partial_lags(phases, channels, table, slice_index, chunk):
    windows, bins_local, _ = phases.shape
    tiles = channels.shape[0]
    cols = 2 * tiles
    flat = channels.reshape(cols, BLOCK)
    columns = flat[:, 0] // LANES
    index = jnp.tile(flat % LANES, (1, LANES // BLOCK))
    out = jax.ShapeDtypeStruct((2, tiles, LAG_ROWS, LANES), jnp.float32)
    pairs = tiles * BLOCK * BLOCK
    whole = pl.BlockSpec(out.shape, lambda i, c, s: (0, 0, 0, 0))

    def raw_spec(m):
        return pl.BlockSpec((windows, chunk, LANES), lambda i, c, s: (0, i, c[m]))

    macs = tiles * bins_local * BLOCK * BLOCK * (windows * 4 + 6 * TAB_ROWS)
    return pl.pallas_call(
        functools.partial(lag_kernel, tiles, windows),
        grid_spec=pltpu.PrefetchScalarGridSpec(
            num_scalar_prefetch=2,
            grid=(bins_local // chunk,),
            in_specs=[raw_spec(m) for m in range(cols)]
            + [
                pl.BlockSpec((cols, LANES), lambda i, c, s: (0, 0)),
                pl.BlockSpec((None, 2, 2, TAB_ROWS, chunk), lambda i, c, s: (s[0], 0, 0, 0, i)),
            ],
            out_specs=[whole, whole],
            scratch_shapes=[pltpu.VMEM((3, windows, cols * BLOCK, LANES), jnp.float32)]
            + [pltpu.VMEM((pairs, chunk), jnp.bfloat16)] * 4
            + [pltpu.VMEM((tiles, 2, TAB_ROWS, BLOCK * BLOCK), jnp.float32)],
        ),
        out_shape=[out, out],
        compiler_params=pltpu.CompilerParams(vmem_limit_bytes=48 * 2**20),
        cost_estimate=pl.CostEstimate(
            flops=2 * macs, bytes_accessed=4 * cols * windows * bins_local * LANES, transcendentals=0
        ),
        name="partial_lags",
    )(columns, slice_index.reshape(1), *([phases] * cols), index, table)


def finish_kernel(*refs):
    out_ref = refs[-1]
    total = refs[0][...]
    for ref in refs[1:-1]:
        total = total + ref[...]
    half = LANES // 2
    other = pltpu.roll(total, half, 1)
    low_lanes = lax.broadcasted_iota(jnp.int32, total.shape, 1) < half
    both = jnp.where(low_lanes, total - other, total + other)
    rows, trailing = out_ref.shape[0], out_ref.shape[1]
    mirror = LANES - 1 - lax.broadcasted_iota(jnp.int32, (half, LANES), 1)
    for k in range(HALF // LANES):
        ahead = both[k * LANES : (k + 1) * LANES, :].T[:half]
        first = HALF + k * LANES
        out_ref[:, :, first : first + LANES] = ahead.reshape(rows, trailing, LANES)
        turned = both[k * LANES + 1 : (k + 1) * LANES + 1, :].T
        behind = jnp.take_along_axis(turned[half:], mirror, axis=1)
        first = HALF - (k + 1) * LANES
        out_ref[:, :, first : first + LANES] = behind.reshape(rows, trailing, LANES)
    last = turned[:half, LANES - 1 :]
    out_ref[:, :, 2 * HALF :] = last.reshape(rows, trailing, 1)


def finish(parts):
    rows = BLOCK // 4
    return pl.pallas_call(
        finish_kernel,
        out_shape=jax.ShapeDtypeStruct((rows, BLOCK, 2 * HALF + 1), jnp.float32),
        name="finish",
    )(*parts)


def by_lags(groups, phases, tile_blocks):
    tile_count = lax.axis_size("tile")
    win_count = lax.axis_size("win")
    windows, bins_local, _ = phases.shape
    place = lax.axis_index("tile")
    me = lax.axis_index("win")
    chip, core = me // 2, me % 2
    table = jnp.asarray(lag_tables(bins_local * tile_count, bins_local, windows * win_count))
    quads = jnp.stack([2 * (chip ^ (r & 1)) + (core ^ (r >> 1)) for r in range(4)])
    lead = (4 * quads[:, None] + jnp.arange(4, dtype=jnp.int32)[None, :]).reshape(BLOCK)
    within = jnp.stack([lead, jnp.arange(BLOCK, dtype=jnp.int32)])

    cross_core = [(w, w ^ 1) for w in range(win_count)]
    cross_chip = [(w, w ^ 2) for w in range(win_count)]
    parts = []
    for group in groups:
        blocks = jnp.stack([tile_blocks[place ^ m] for m in group])
        channels = blocks[:, :, None] * BLOCK + within[None]
        keep, send = partial_lags(phases, channels, table, place, 256)
        came = lax.ppermute(send, "win", cross_core)
        away = keep[1] + came[1]
        mine = keep[0] + came[0]
        mine = mine + lax.ppermute(away, "win", cross_chip)
        for k, m in enumerate(group):
            part = mine[k]
            if m:
                part = lax.ppermute(part, "tile", [(z, z ^ m) for z in range(tile_count)])
            parts.append(part)
    return finish(parts)[None]


def tables_at(freq_index, bin_count, half_lags, windows):
    freq_index = freq_index[:, None]
    lag_index = jnp.arange(2 * half_lags + 1, dtype=jnp.int32)[None, :] - half_lags
    phase_turns = jnp.mod(freq_index * lag_index, 2 * bin_count).astype(jnp.float32)
    angles = phase_turns * jnp.float32(math.pi / bin_count)
    weight = jnp.where(freq_index == 0, 1.0, 2.0).astype(jnp.float32) / jnp.float32(
        math.sqrt(2.0 * windows * bin_count)
    )
    return (weight * jnp.cos(angles), -weight * jnp.sin(angles))


def cross_spectra(leading, trailing):
    cos_lead, sin_lead = (jnp.cos(leading), jnp.sin(leading))
    cos_trail, sin_trail = (jnp.cos(trailing), jnp.sin(trailing))
    highest = lax.Precision.HIGHEST
    cross_real = jnp.einsum("wfi,wfj->fij", cos_lead, cos_trail, precision=highest) + jnp.einsum(
        "wfi,wfj->fij", sin_lead, sin_trail, precision=highest
    )
    cross_imag = jnp.einsum("wfi,wfj->fij", sin_lead, cos_trail, precision=highest) - jnp.einsum(
        "wfi,wfj->fij", cos_lead, sin_trail, precision=highest
    )
    return (cross_real, cross_imag)


def to_lags(cross_real, cross_imag, cos_tab, sin_tab):
    bin_count, rows_a, rows_b = cross_real.shape
    dims = (((0,), (0,)), ((), ()))
    highest = lax.Precision.HIGHEST
    lagged = lax.dot_general(
        cross_real.reshape(bin_count, rows_a * rows_b), cos_tab, dims, precision=highest
    )
    lagged = lagged + lax.dot_general(
        cross_imag.reshape(bin_count, rows_a * rows_b), sin_tab, dims, precision=highest
    )
    return lagged.reshape(rows_a, rows_b, cos_tab.shape[1])


def by_phases(phases, tile_blocks):
    tile_count = lax.axis_size("tile")
    win_count = lax.axis_size("win")
    win_local = phases.shape[0]
    bins_local = phases.shape[1]
    total_bins = bins_local * tile_count
    total_windows = win_local * win_count
    offsets = jnp.arange(BLOCK, dtype=jnp.int32)
    channels = (tile_blocks[:, :, None] * BLOCK + offsets[None, None, :]).reshape(
        tile_count * 2 * BLOCK
    )
    chosen = jnp.take(phases, channels, axis=2)
    quarter = bins_local // win_count
    received = lax.all_to_all(chosen, "tile", split_axis=2, concat_axis=1, tiled=True)
    shaped = received.reshape(win_local, tile_count, win_count, quarter, 2 * BLOCK)
    arrived = lax.all_to_all(shaped, "win", split_axis=2, concat_axis=0, tiled=True)
    arrived = arrived.reshape(total_windows, tile_count * quarter, 2 * BLOCK)
    source_index = jnp.arange(tile_count, dtype=jnp.int32)[:, None]
    inner_index = jnp.arange(quarter, dtype=jnp.int32)[None, :]
    freq_index = (
        source_index * bins_local + lax.axis_index("win") * quarter + inner_index
    ).reshape(tile_count * quarter)
    cos_tab, sin_tab = tables_at(freq_index, total_bins, HALF, total_windows)
    cross_real, cross_imag = cross_spectra(arrived[:, :, :BLOCK], arrived[:, :, BLOCK:])
    partial_lags = to_lags(cross_real, cross_imag, cos_tab, sin_tab)
    lagged = lax.psum_scatter(partial_lags, "win", scatter_dimension=0, tiled=True)
    return lagged[None]


def on_device(groups, phases, tile_blocks):
    tile_count = lax.axis_size("tile")
    windows, bins_local, _ = phases.shape
    lag_values = tile_count * BLOCK * BLOCK * (2 * HALF + 1)
    phase_values = tile_count * 2 * BLOCK * windows * bins_local
    fits = (
        lax.axis_size("win") == 4
        and tile_count & (tile_count - 1) == 0
        and bins_local % 256 == 0
        and windows % 8 == 0
        and phases.shape[2] % LANES == 0
    )
    if fits and lag_values < phase_values:
        return by_lags(groups, phases, tile_blocks)
    return by_phases(phases, tile_blocks)


def solution(mesh):
    placed = (P(("groups", "win"), "tile", None), P())
    groups = [[m] for m in reversed(range(mesh.shape["tile"]))]
    return jax.shard_map(
        functools.partial(on_device, groups),
        mesh=mesh,
        in_specs=placed,
        out_specs=P(("groups", "tile"), "win", None, None),
        check_vma=False,
    )
```

```python
import functools
import math

import jax
import jax.numpy as jnp
import numpy as np
from jax import lax
from jax.experimental import pallas as pl
from jax.experimental.pallas import tpu as pltpu
from jax.sharding import PartitionSpec as P

BLOCK = 16
HALF = 256
LANES = 128
TAB_ROWS = 272
LAG_ROWS = 264
SIN_FIT = (7.0710677816e-01, -2.9462767175e-02, 3.6827228729e-04, -2.1886110623e-06, 7.1958213082e-09)
COS_FIT = (1.4142134963e+00, -1.7677635964e-01, 3.6825748950e-03, -3.0612567514e-05, 1.2790438412e-07)


def lag_tables(total_bins, bins_local, windows):
    bins = np.arange(total_bins, dtype=np.int64)
    lags = np.arange(TAB_ROWS, dtype=np.int64)
    angles = np.mod(lags[:, None] * bins[None, :], 2 * total_bins) * (math.pi / total_bins)
    weight = np.where(bins == 0, 1.0, 2.0) / math.sqrt(2.0 * windows * total_bins)
    out = []
    for values in (weight * np.cos(angles), weight * np.sin(angles)):
        values = values.astype(np.float32)
        high = values.astype(jnp.bfloat16)
        low = (values - high.astype(np.float32)).astype(jnp.bfloat16)
        out.append(np.stack([high, low]))
    table = np.stack(out)
    table = table.reshape(2, 2, TAB_ROWS, total_bins // bins_local, bins_local)
    return np.ascontiguousarray(np.moveaxis(table, 3, 0))


def horner(coefs, z):
    acc = z * coefs[-1] + coefs[-2]
    for coef in coefs[-3::-1]:
        acc = acc * z + coef
    return acc


def sin_cos(x):
    z = x * x
    t = x * horner(SIN_FIT, z)
    q = horner(COS_FIT, z)
    return t * q, 1.0 - t * t


def lag_kernel(group, windows, place_ref, blocks_ref, *refs):
    tiles = len(group)
    cols = 2 * tiles
    raw_refs = refs[:cols]
    tab_ref, keep_ref, send_ref = refs[cols : cols + 3]
    planes = refs[cols + 3 : cols + 5]
    spectra = refs[cols + 5 : cols + 7]
    acc_ref = refs[cols + 7]
    step = pl.program_id(0)
    last = pl.num_programs(0) - 1
    pairs = BLOCK * BLOCK
    per_vec = LANES // (cols * BLOCK)
    lane = lax.broadcasted_iota(jnp.int32, (LANES, LANES), 1)
    slots = [(w, m) for w in range(per_vec) for m in range(cols)]

    def lane_index(m):
        at = lane[:8] % BLOCK
        if m % 2 == 0:
            chip, core = place_ref[1] // 2, place_ref[1] % 2
            turned = ((at // 8) ^ core) * 4 + (((at // 4) % 2) ^ chip) * 8
            at = turned + at % 4
        block = blocks_ref[place_ref[0] ^ group[m // 2], m % 2]
        row = at + (block % (LANES // BLOCK)) * BLOCK
        return jnp.tile(row, (LANES // 8, 1))

    def front(unit):
        index = [lane_index(m) for m in range(cols)]

        def one(group_index):
            packed = None
            for slot, (w, m) in enumerate(slots):
                rows = pl.ds(unit * LANES, LANES)
                raw = raw_refs[m][group_index * per_vec + w, rows, :]
                moved = jnp.take_along_axis(raw, index[m], axis=1)
                packed = moved if packed is None else jnp.where(lane >= slot * BLOCK, moved, packed)
            sin, cos = sin_cos(packed.T)
            both = cos + sin
            diff = cos - sin
            for slot, (w, m) in enumerate(slots):
                part = slice(slot * BLOCK, (slot + 1) * BLOCK)
                three = (both, sin, cos) if m % 2 == 0 else (cos, diff, both)
                for p in range(3):
                    where = (p, group_index * per_vec + w, slice(m * BLOCK, (m + 1) * BLOCK))
                    planes[unit][where] = three[p][part]

        return [functools.partial(one, g) for g in range(windows // per_vec)]

    def cross(unit):
        def one(tile, quad):
            lead, trail = 2 * tile * BLOCK, (2 * tile + 1) * BLOCK
            sums = [[None] * 3 for _ in range(4)]
            for w in range(windows):
                for p in range(3):
                    right = planes[unit][p, w, trail : trail + BLOCK, :]
                    for i in range(4):
                        row = lead + quad * 4 + i
                        prod = planes[unit][p, w, row : row + 1, :] * right
                        sums[i][p] = prod if w == 0 else sums[i][p] + prod
            for i in range(4):
                first = (quad * 4 + i) * BLOCK
                for part in range(2):
                    value = sums[i][0] - sums[i][1 + part]
                    high = value.astype(jnp.bfloat16)
                    low = (value - high.astype(jnp.float32)).astype(jnp.bfloat16)
                    spectra[unit][tile, part, first : first + BLOCK, :LANES] = high
                    spectra[unit][tile, part, first : first + BLOCK, LANES:] = low

        return [functools.partial(one, t, q) for t in range(tiles) for q in range(BLOCK // 4)]

    def lags(unit):
        def product(table, values):
            return lax.dot_general(
                table, values, (((1,), (1,)), ((), ())), preferred_element_type=jnp.float32
            )

        def one(tile, part):
            bins = slice(unit * LANES, (unit + 1) * LANES)
            high, low = tab_ref[part, 0, :, bins], tab_ref[part, 1, :, bins]
            values = spectra[unit][tile, part]
            total = product(jnp.concatenate([high, high], axis=1), values)
            acc_ref[tile, part] += total + product(low, values[:, :LANES])

        return [functools.partial(one, t, part) for t in range(tiles) for part in range(2)]

    def run(*stages):
        pieces = []
        for stage in stages:
            pieces += [((k + 0.5) / len(stage), n, piece) for k, (n, piece) in enumerate(zip(range(99), stage))]
        for _, _, piece in sorted(pieces, key=lambda entry: entry[:2]):
            piece()

    @pl.when(step == 0)
    def _():
        acc_ref[...] = jnp.zeros_like(acc_ref)
        spectra[1][...] = jnp.zeros_like(spectra[1])
        run(front(0))

    @pl.when((step > 0) & (step < last))
    def _():
        run(front(0), cross(1), lags(0))

    @pl.when(step < last)
    def _():
        run(front(1), cross(0), lags(1))

    @pl.when(step == last)
    def _():
        run(cross(1), lags(0))
        run(lags(1))
        half = LANES // 2
        low_lanes = lax.broadcasted_iota(jnp.int32, (LAG_ROWS, LANES), 1) < half
        for tile in range(tiles):
            for core, ref in enumerate((keep_ref, send_ref)):
                cut = (slice(0, LAG_ROWS), slice(core * LANES, (core + 1) * LANES))
                even, odd = acc_ref[(tile, 0) + cut], acc_ref[(tile, 1) + cut]
                ref[0, tile] = jnp.where(low_lanes, even, pltpu.roll(odd, half, 1))
                ref[1, tile] = jnp.where(low_lanes, pltpu.roll(even, half, 1), odd)


def partial_lags(group, phases, tile_blocks, table, place):
    windows, bins_local, _ = phases.shape
    tiles = len(group)
    cols = 2 * tiles
    chunk = 2 * LANES
    steps = bins_local // chunk
    pairs = BLOCK * BLOCK
    per_lane_tile = LANES // BLOCK
    out = jax.ShapeDtypeStruct((2, tiles, LAG_ROWS, LANES), jnp.float32)
    whole = pl.BlockSpec(out.shape, lambda i, p, b: (0, 0, 0, 0))

    def raw_spec(m):
        def where(i, p, b):
            return 0, jnp.minimum(i, steps - 1), b[p[0] ^ group[m // 2], m % 2] // per_lane_tile

        return pl.BlockSpec((windows, chunk, LANES), where)

    def table_at(i, p, b):
        return p[0], 0, 0, 0, jnp.maximum(i - 1, 0)

    macs = tiles * bins_local * pairs * (windows * 4 + 6 * TAB_ROWS)
    return pl.pallas_call(
        functools.partial(lag_kernel, group, windows),
        grid_spec=pltpu.PrefetchScalarGridSpec(
            num_scalar_prefetch=2,
            grid=(steps + 1,),
            in_specs=[raw_spec(m) for m in range(cols)]
            + [pl.BlockSpec((None, 2, 2, TAB_ROWS, chunk), table_at)],
            out_specs=[whole, whole],
            scratch_shapes=[pltpu.VMEM((3, windows, cols * BLOCK, LANES), jnp.float32)] * 2
            + [pltpu.VMEM((tiles, 2, pairs, 2 * LANES), jnp.bfloat16)] * 2
            + [pltpu.VMEM((tiles, 2, TAB_ROWS, pairs), jnp.float32)],
        ),
        out_shape=[out, out],
        compiler_params=pltpu.CompilerParams(vmem_limit_bytes=40 * 2**20),
        cost_estimate=pl.CostEstimate(
            flops=2 * macs, bytes_accessed=4 * cols * windows * bins_local * LANES, transcendentals=0
        ),
        name="partial_lags",
    )(place, tile_blocks, *([phases] * cols), table)


def finish_kernel(*refs):
    out_ref = refs[-1]
    total = refs[0][...]
    for ref in refs[1:-1]:
        total = total + ref[...]
    half = LANES // 2
    other = pltpu.roll(total, half, 1)
    low_lanes = lax.broadcasted_iota(jnp.int32, total.shape, 1) < half
    both = jnp.where(low_lanes, total - other, total + other)
    rows, trailing = out_ref.shape[0], out_ref.shape[1]
    mirror = LANES - 1 - lax.broadcasted_iota(jnp.int32, (half, LANES), 1)
    for k in range(HALF // LANES):
        ahead = both[k * LANES : (k + 1) * LANES, :].T[:half]
        first = HALF + k * LANES
        out_ref[:, :, first : first + LANES] = ahead.reshape(rows, trailing, LANES)
        turned = both[k * LANES + 1 : (k + 1) * LANES + 1, :].T
        behind = jnp.take_along_axis(turned[half:], mirror, axis=1)
        first = HALF - (k + 1) * LANES
        out_ref[:, :, first : first + LANES] = behind.reshape(rows, trailing, LANES)
    last = turned[:half, LANES - 1 :]
    out_ref[:, :, 2 * HALF :] = last.reshape(rows, trailing, 1)


def finish(parts):
    rows = BLOCK // 4
    return pl.pallas_call(
        finish_kernel,
        out_shape=jax.ShapeDtypeStruct((rows, BLOCK, 2 * HALF + 1), jnp.float32),
        name="finish",
    )(*parts)


def by_lags(groups, phases, tile_blocks):
    tile_count = lax.axis_size("tile")
    win_count = lax.axis_size("win")
    windows, bins_local, _ = phases.shape
    place = jnp.stack([lax.axis_index("tile"), lax.axis_index("win")])
    table = jnp.asarray(lag_tables(bins_local * tile_count, bins_local, windows * win_count))
    cross_core = [(w, w ^ 1) for w in range(win_count)]
    cross_chip = [(w, w ^ 2) for w in range(win_count)]
    parts = []
    for group in groups:
        keep, send = partial_lags(group, phases, tile_blocks, table, place)
        came = lax.ppermute(send, "win", cross_core)
        away = keep[1] + came[1]
        mine = keep[0] + came[0]
        mine = mine + lax.ppermute(away, "win", cross_chip)
        for k, m in enumerate(group):
            part = mine[k]
            if m:
                part = lax.ppermute(part, "tile", [(z, z ^ m) for z in range(tile_count)])
            parts.append(part)
    return finish(parts)[None]


def tables_at(freq_index, bin_count, half_lags, windows):
    freq_index = freq_index[:, None]
    lag_index = jnp.arange(2 * half_lags + 1, dtype=jnp.int32)[None, :] - half_lags
    phase_turns = jnp.mod(freq_index * lag_index, 2 * bin_count).astype(jnp.float32)
    angles = phase_turns * jnp.float32(math.pi / bin_count)
    weight = jnp.where(freq_index == 0, 1.0, 2.0).astype(jnp.float32) / jnp.float32(
        math.sqrt(2.0 * windows * bin_count)
    )
    return (weight * jnp.cos(angles), -weight * jnp.sin(angles))


def cross_spectra(leading, trailing):
    cos_lead, sin_lead = (jnp.cos(leading), jnp.sin(leading))
    cos_trail, sin_trail = (jnp.cos(trailing), jnp.sin(trailing))
    highest = lax.Precision.HIGHEST
    cross_real = jnp.einsum("wfi,wfj->fij", cos_lead, cos_trail, precision=highest) + jnp.einsum(
        "wfi,wfj->fij", sin_lead, sin_trail, precision=highest
    )
    cross_imag = jnp.einsum("wfi,wfj->fij", sin_lead, cos_trail, precision=highest) - jnp.einsum(
        "wfi,wfj->fij", cos_lead, sin_trail, precision=highest
    )
    return (cross_real, cross_imag)


def to_lags(cross_real, cross_imag, cos_tab, sin_tab):
    bin_count, rows_a, rows_b = cross_real.shape
    dims = (((0,), (0,)), ((), ()))
    highest = lax.Precision.HIGHEST
    lagged = lax.dot_general(
        cross_real.reshape(bin_count, rows_a * rows_b), cos_tab, dims, precision=highest
    )
    lagged = lagged + lax.dot_general(
        cross_imag.reshape(bin_count, rows_a * rows_b), sin_tab, dims, precision=highest
    )
    return lagged.reshape(rows_a, rows_b, cos_tab.shape[1])


def by_phases(phases, tile_blocks):
    tile_count = lax.axis_size("tile")
    win_count = lax.axis_size("win")
    win_local = phases.shape[0]
    bins_local = phases.shape[1]
    total_bins = bins_local * tile_count
    total_windows = win_local * win_count
    offsets = jnp.arange(BLOCK, dtype=jnp.int32)
    channels = (tile_blocks[:, :, None] * BLOCK + offsets[None, None, :]).reshape(
        tile_count * 2 * BLOCK
    )
    chosen = jnp.take(phases, channels, axis=2)
    quarter = bins_local // win_count
    received = lax.all_to_all(chosen, "tile", split_axis=2, concat_axis=1, tiled=True)
    shaped = received.reshape(win_local, tile_count, win_count, quarter, 2 * BLOCK)
    arrived = lax.all_to_all(shaped, "win", split_axis=2, concat_axis=0, tiled=True)
    arrived = arrived.reshape(total_windows, tile_count * quarter, 2 * BLOCK)
    source_index = jnp.arange(tile_count, dtype=jnp.int32)[:, None]
    inner_index = jnp.arange(quarter, dtype=jnp.int32)[None, :]
    freq_index = (
        source_index * bins_local + lax.axis_index("win") * quarter + inner_index
    ).reshape(tile_count * quarter)
    cos_tab, sin_tab = tables_at(freq_index, total_bins, HALF, total_windows)
    cross_real, cross_imag = cross_spectra(arrived[:, :, :BLOCK], arrived[:, :, BLOCK:])
    partial_lags = to_lags(cross_real, cross_imag, cos_tab, sin_tab)
    lagged = lax.psum_scatter(partial_lags, "win", scatter_dimension=0, tiled=True)
    return lagged[None]


def on_device(groups, phases, tile_blocks):
    tile_count = lax.axis_size("tile")
    windows, bins_local, _ = phases.shape
    lag_values = tile_count * BLOCK * BLOCK * (2 * HALF + 1)
    phase_values = tile_count * 2 * BLOCK * windows * bins_local
    fits = (
        lax.axis_size("win") == 4
        and tile_count & (tile_count - 1) == 0
        and bins_local % 256 == 0
        and windows % 8 == 0
        and phases.shape[2] % LANES == 0
    )
    if fits and lag_values < phase_values:
        return by_lags(groups, phases, tile_blocks)
    return by_phases(phases, tile_blocks)


def solution(mesh):
    placed = (P(("groups", "win"), "tile", None), P())
    order = list(reversed(range(mesh.shape["tile"])))
    groups = [order[k : k + 2] for k in range(0, len(order), 2)]
    return jax.shard_map(
        functools.partial(on_device, groups),
        mesh=mesh,
        in_specs=placed,
        out_specs=P(("groups", "tile"), "win", None, None),
        check_vma=False,
    )
```

```python
import functools
import math

import jax
import jax.numpy as jnp
import numpy as np
from jax import lax
from jax.experimental import pallas as pl
from jax.experimental.pallas import tpu as pltpu
from jax.sharding import PartitionSpec as P

BLOCK = 16
HALF = 256
LANES = 128
TAB_ROWS = 272
FRONT_VMEM = 50 * 2**20
LAG_VMEM = 50 * 2**20
LAG_ROWS = 264
SIN_FIT = (7.0710677816e-01, -2.9462767175e-02, 3.6827228729e-04, -2.1886110623e-06, 7.1958213082e-09)
COS_FIT = (1.4142134963e+00, -1.7677635964e-01, 3.6825748950e-03, -3.0612567514e-05, 1.2790438412e-07)


def lag_tables(total_bins, bins_local, windows):
    bins = np.arange(total_bins, dtype=np.int64)
    lags = np.arange(TAB_ROWS, dtype=np.int64)
    angles = np.mod(lags[:, None] * bins[None, :], 2 * total_bins) * (math.pi / total_bins)
    weight = np.where(bins == 0, 1.0, 2.0) / math.sqrt(2.0 * windows * total_bins)
    out = []
    for values in (weight * np.cos(angles), weight * np.sin(angles)):
        values = values.astype(np.float32)
        high = values.astype(jnp.bfloat16)
        low = (values - high.astype(np.float32)).astype(jnp.bfloat16)
        out.append(np.stack([high, low]))
    table = np.stack(out)
    table = table.reshape(2, 2, TAB_ROWS, total_bins // bins_local, bins_local)
    return np.ascontiguousarray(np.moveaxis(table, 3, 0))


def horner(coefs, z):
    acc = z * coefs[-1] + coefs[-2]
    for coef in coefs[-3::-1]:
        acc = acc * z + coef
    return acc


def sin_cos(x):
    z = x * x
    t = x * horner(SIN_FIT, z)
    q = horner(COS_FIT, z)
    return t * q, 1.0 - t * t


def front_kernel(tiles, ids_ref, phases_ref, tables_ref, out_ref, tab_ref, *refs):
    raw_ref, stage_ref, packed, turned = refs[0], refs[1], refs[2:4], refs[4:6]
    raw_sem, stage_sem, tab_sem = refs[6:]
    table_copy = pltpu.make_async_copy(tables_ref.at[ids_ref[0]], tab_ref, tab_sem)
    windows, bins_local, channels = raw_ref.shape
    units = bins_local // LANES
    per_lane_tile = LANES // BLOCK

    def raw_copy(unit):
        bins = pl.ds(unit * LANES, LANES)
        return pltpu.make_async_copy(phases_ref.at[:, bins, :], raw_ref.at[:, bins, :], raw_sem.at[unit])

    for unit in range(units):
        raw_copy(unit).start()
    table_copy.start()

    def stage_copy(unit):
        slot = unit % 2
        return pltpu.make_async_copy(stage_ref.at[slot], out_ref.at[:, unit], stage_sem.at[slot])

    lane = lax.broadcasted_iota(jnp.int32, (8, LANES), 1)
    at, col = lane % BLOCK, lane // BLOCK
    chip, core = ids_ref[1] // 2, ids_ref[1] % 2
    lead = ((at // 8) ^ core) * 4 + (((at // 4) % 2) ^ chip) * 8 + at % 4
    block = jnp.zeros_like(lane)
    for m in range(2 * tiles):
        block = jnp.where(col == m, ids_ref[2 + 2 * (ids_ref[0] ^ (m // 2)) + m % 2], block)
    row = jnp.where(col % 2 == 0, lead, at) + (block % per_lane_tile) * BLOCK
    row = jnp.tile(row, (BLOCK // 8, 1))
    source = jnp.tile(block // per_lane_tile, (BLOCK // 8, 1))

    def gather(item, to, piece):
        unit, w = item // windows, item % windows
        first = pl.multiple_of(unit * LANES + piece * BLOCK, BLOCK)
        value = None
        for q in range(channels // LANES):
            raw = raw_ref[w, pl.ds(first, BLOCK), q * LANES : (q + 1) * LANES]
            moved = jnp.take_along_axis(raw, row, axis=1)
            value = moved if value is None else jnp.where(source == q, moved, value)
        to[piece * BLOCK : (piece + 1) * BLOCK] = value

    def unfold(item, rows_ref, m):
        unit, w = item // windows, item % windows
        sin, cos = sin_cos(rows_ref[m * BLOCK : (m + 1) * BLOCK])
        stage_ref[unit % 2, m // 2, 0, w, m % 2] = cos
        stage_ref[unit % 2, m // 2, 1, w, m % 2] = sin

    pieces = range(LANES // BLOCK)
    raw_copy(0).wait()
    for piece in pieces:
        gather(0, packed[1], piece)
    turned[0][...] = packed[1][...].T
    for piece in pieces:
        gather(1, packed[0], piece)

    @pl.loop(0, units)
    def _(unit):
        @pl.when(unit + 1 < units)
        def _():
            raw_copy(unit + 1).wait()

        @pl.when(unit >= 2)
        def _():
            stage_copy(unit - 2).wait()

        @pl.loop(0, windows // 4)
        def _(h):
            for j in range(4):
                item = unit * windows + 4 * h + j
                here, there = j % 2, 1 - j % 2
                turned[there][...] = packed[here][...].T
                for piece in pieces:
                    gather(jnp.minimum(item + 2, units * windows - 1), packed[there], piece)
                    unfold(item, turned[here], piece)

        stage_copy(unit).start()

    table_copy.wait()
    for unit in range(units - 2, units):
        stage_copy(unit).wait()


def waves_of(phases, ids, tables, tiles):
    windows, bins_local, channels = phases.shape
    table = jax.ShapeDtypeStruct(tables.shape[1:], tables.dtype)
    out = jax.ShapeDtypeStruct((tiles, bins_local // LANES, 2, windows, 2, BLOCK, LANES), jnp.float32)
    smem, vmem = pl.BlockSpec(memory_space=pltpu.SMEM), pl.BlockSpec(memory_space=pltpu.VMEM)
    return pl.pallas_call(
        functools.partial(front_kernel, tiles),
        in_specs=[smem] + [pl.BlockSpec(memory_space=pl.ANY)] * 2,
        out_specs=[pl.BlockSpec(memory_space=pl.ANY), vmem],
        out_shape=[out, table],
        scratch_shapes=[
            pltpu.VMEM(phases.shape, jnp.float32),
            pltpu.VMEM((2, tiles) + out.shape[2:], jnp.float32),
        ]
        + [pltpu.VMEM((LANES, LANES), jnp.float32)] * 4
        + [pltpu.SemaphoreType.DMA((k,)) for k in (bins_local // LANES, 2)]
        + [pltpu.SemaphoreType.DMA],
        compiler_params=pltpu.CompilerParams(vmem_limit_bytes=FRONT_VMEM),
        cost_estimate=pl.CostEstimate(flops=10**10, bytes_accessed=phases.size * 4, transcendentals=0),
        name="waves",
    )(ids, phases, tables)


def lag_kernel(m, after_ref, waves_ref, tab_ref, keep_ref, send_ref, wave_ref, acc_ref, plane_ref, *scratch):
    del after_ref
    spectra, wave_sem = scratch[:2], scratch[2]
    units, _, windows = wave_ref.shape[:3]

    def wave_copy(unit):
        return pltpu.make_async_copy(waves_ref.at[m, unit], wave_ref.at[unit], wave_sem.at[unit])

    for unit in range(units):
        wave_copy(unit).start()

    subs = spectra[0].shape[0]
    chunks = units // subs

    def prepare(unit):
        for w in range(windows):
            lead_cos, trail_cos = wave_ref[unit, 0, w, 0], wave_ref[unit, 0, w, 1]
            lead_sin, trail_sin = wave_ref[unit, 1, w, 0], wave_ref[unit, 1, w, 1]
            plane_ref[0, w, 0], plane_ref[1, w, 0], plane_ref[2, w, 0] = lead_cos + lead_sin, lead_sin, lead_cos
            plane_ref[0, w, 1], plane_ref[1, w, 1] = trail_cos, trail_cos - trail_sin
            plane_ref[2, w, 1] = trail_cos + trail_sin

    def cross(sub, parity, quads):
        for quad in quads:
            sums = [[None] * 3 for _ in range(4)]
            for w in range(windows):
                for p in range(3):
                    right = plane_ref[p, w, 1]
                    for i in range(4):
                        row = quad * 4 + i
                        prod = plane_ref[p, w, 0, row : row + 1, :] * right
                        sums[i][p] = prod if w == 0 else sums[i][p] + prod
            for i in range(4):
                rows = slice((quad * 4 + i) * BLOCK, (quad * 4 + i + 1) * BLOCK)
                for part in range(2):
                    value = sums[i][0] - sums[i][1 + part]
                    high = value.astype(jnp.bfloat16)
                    low = value - high.astype(jnp.float32)
                    spectra[parity][sub, part, 0, rows] = high
                    spectra[parity][sub, part, 1, rows] = low.astype(jnp.bfloat16)

    def product(table, values):
        return lax.dot_general(
            table, values, (((1,), (1,)), ((), ())), preferred_element_type=jnp.float32
        )

    def lags(k, part, parity):
        bins = pl.ds(pl.multiple_of(k * subs * LANES, subs * LANES), subs * LANES)
        high, low = (
            jnp.concatenate([spectra[parity][sub, part, half] for sub in range(subs)], axis=1)
            for half in range(2)
        )
        tab_high, tab_low = tab_ref[part, 0, :, bins], tab_ref[part, 1, :, bins]
        total = product(tab_high, high) + product(tab_low, high) + product(tab_high, low)
        acc_ref[part] += total

    acc_ref[...] = jnp.zeros_like(acc_ref)
    spectra[1][...] = jnp.zeros_like(spectra[1])

    @pl.loop(0, chunks // 2)
    def _(k):
        for parity in range(2):

            @pl.loop(0, 2)
            def _(g):
                unit = (2 * k + parity) * subs + g
                wave_copy(unit).wait()
                prepare(unit)
                cross(g, parity, (0, 1))
                lags(jnp.maximum(2 * k + parity - 1, 0), g, 1 - parity)
                cross(g, parity, (2, 3))

    for part in range(2):
        lags(chunks - 1, part, 1)
    middle = LANES // 2
    low_lanes = lax.broadcasted_iota(jnp.int32, (LAG_ROWS, LANES), 1) < middle
    for core, ref in enumerate((keep_ref, send_ref)):
        cut = (slice(0, LAG_ROWS), slice(core * LANES, (core + 1) * LANES))
        even, odd = acc_ref[(0,) + cut], acc_ref[(1,) + cut]
        ref[0] = jnp.where(low_lanes, even, pltpu.roll(odd, middle, 1))
        ref[1] = jnp.where(low_lanes, pltpu.roll(even, middle, 1), odd)


def partial_lags(m, waves, table, after):
    pairs = BLOCK * BLOCK
    planes = pltpu.VMEM((3,) + waves.shape[3:], jnp.float32)
    out = jax.ShapeDtypeStruct((2, LAG_ROWS, LANES), jnp.float32)
    vmem = pl.BlockSpec(memory_space=pltpu.VMEM)
    return pl.pallas_call(
        functools.partial(lag_kernel, m),
        in_specs=[pl.BlockSpec(memory_space=pltpu.SMEM), pl.BlockSpec(memory_space=pl.ANY), vmem],
        out_specs=[vmem, vmem],
        out_shape=[out, out],
        scratch_shapes=[
            pltpu.VMEM(waves.shape[1:], jnp.float32),
            pltpu.VMEM((2, TAB_ROWS, pairs), jnp.float32),
            planes,
        ]
        + [pltpu.VMEM((2, 2, 2, pairs, LANES), jnp.bfloat16)] * 2
        + [pltpu.SemaphoreType.DMA(waves.shape[1:2])],
        compiler_params=pltpu.CompilerParams(vmem_limit_bytes=LAG_VMEM),
        cost_estimate=pl.CostEstimate(flops=4 * 10**9, bytes_accessed=waves.size, transcendentals=0),
        name="partial_lags",
    )(after, waves, table)


def finish_kernel(*refs):
    out_ref = refs[-1]
    total = refs[0][...]
    for ref in refs[1:-1]:
        total = total + ref[...]
    half = LANES // 2
    other = pltpu.roll(total, half, 1)
    low_lanes = lax.broadcasted_iota(jnp.int32, total.shape, 1) < half
    both = jnp.where(low_lanes, total - other, total + other)
    rows, trailing = out_ref.shape[0], out_ref.shape[1]
    mirror = LANES - 1 - lax.broadcasted_iota(jnp.int32, (half, LANES), 1)
    for k in range(HALF // LANES):
        ahead = both[k * LANES : (k + 1) * LANES, :].T[:half]
        first = HALF + k * LANES
        out_ref[:, :, first : first + LANES] = ahead.reshape(rows, trailing, LANES)
        turned = both[k * LANES + 1 : (k + 1) * LANES + 1, :].T
        behind = jnp.take_along_axis(turned[half:], mirror, axis=1)
        first = HALF - (k + 1) * LANES
        out_ref[:, :, first : first + LANES] = behind.reshape(rows, trailing, LANES)
    last = turned[:half, LANES - 1 :]
    out_ref[:, :, 2 * HALF :] = last.reshape(rows, trailing, 1)


def finish(parts):
    rows = BLOCK // 4
    return pl.pallas_call(
        finish_kernel,
        out_shape=jax.ShapeDtypeStruct((rows, BLOCK, 2 * HALF + 1), jnp.float32),
        name="finish",
    )(*parts)


def by_lags(phases, tile_blocks):
    tile_count = lax.axis_size("tile")
    win_count = lax.axis_size("win")
    windows, bins_local, _ = phases.shape
    place = jnp.stack([lax.axis_index("tile"), lax.axis_index("win")])
    ids = jnp.concatenate([place, tile_blocks.reshape(-1)])
    tables = jnp.asarray(lag_tables(bins_local * tile_count, bins_local, windows * win_count))
    cross_core = [(w, w ^ 1) for w in range(win_count)]
    cross_chip = [(w, w ^ 2) for w in range(win_count)]
    waves, table = waves_of(phases, ids, tables, tile_count)
    after = ids[:1]
    keep, came, away, part = {}, {}, {}, {}

    def over_core(m):
        keep[m], send = partial_lags(m, waves, table, after)
        came[m] = lax.ppermute(send, "win", cross_core)

    def over_chip(m):
        part[m] = keep[m][0] + came[m][0] + lax.ppermute(away[m], "win", cross_chip)

    def over_tile(m):
        part[m] = lax.ppermute(part[m], "tile", [(z, z ^ m) for z in range(tile_count)])

    over_core(3)
    over_core(2)
    away[3] = keep[3][1] + came[3][1]
    after, away[3] = lax.optimization_barrier((after, away[3]))
    over_chip(3)
    over_core(1)
    away[2] = keep[2][1] + came[2][1]
    after, away[2], part[3] = lax.optimization_barrier((after, away[2], part[3]))
    over_chip(2)
    over_tile(3)
    over_core(0)
    over_tile(2)
    for m in (1, 0):
        away[m] = keep[m][1] + came[m][1]
        over_chip(m)
    over_tile(1)
    parts = [part[m] for m in (3, 2, 1, 0)]
    return finish(parts)[None]


def tables_at(freq_index, bin_count, half_lags, windows):
    freq_index = freq_index[:, None]
    lag_index = jnp.arange(2 * half_lags + 1, dtype=jnp.int32)[None, :] - half_lags
    phase_turns = jnp.mod(freq_index * lag_index, 2 * bin_count).astype(jnp.float32)
    angles = phase_turns * jnp.float32(math.pi / bin_count)
    weight = jnp.where(freq_index == 0, 1.0, 2.0).astype(jnp.float32) / jnp.float32(
        math.sqrt(2.0 * windows * bin_count)
    )
    return (weight * jnp.cos(angles), -weight * jnp.sin(angles))


def cross_spectra(leading, trailing):
    cos_lead, sin_lead = (jnp.cos(leading), jnp.sin(leading))
    cos_trail, sin_trail = (jnp.cos(trailing), jnp.sin(trailing))
    highest = lax.Precision.HIGHEST
    cross_real = jnp.einsum("wfi,wfj->fij", cos_lead, cos_trail, precision=highest) + jnp.einsum(
        "wfi,wfj->fij", sin_lead, sin_trail, precision=highest
    )
    cross_imag = jnp.einsum("wfi,wfj->fij", sin_lead, cos_trail, precision=highest) - jnp.einsum(
        "wfi,wfj->fij", cos_lead, sin_trail, precision=highest
    )
    return (cross_real, cross_imag)


def to_lags(cross_real, cross_imag, cos_tab, sin_tab):
    bin_count, rows_a, rows_b = cross_real.shape
    dims = (((0,), (0,)), ((), ()))
    highest = lax.Precision.HIGHEST
    lagged = lax.dot_general(
        cross_real.reshape(bin_count, rows_a * rows_b), cos_tab, dims, precision=highest
    )
    lagged = lagged + lax.dot_general(
        cross_imag.reshape(bin_count, rows_a * rows_b), sin_tab, dims, precision=highest
    )
    return lagged.reshape(rows_a, rows_b, cos_tab.shape[1])


def by_phases(phases, tile_blocks):
    tile_count = lax.axis_size("tile")
    win_count = lax.axis_size("win")
    win_local = phases.shape[0]
    bins_local = phases.shape[1]
    total_bins = bins_local * tile_count
    total_windows = win_local * win_count
    offsets = jnp.arange(BLOCK, dtype=jnp.int32)
    channels = (tile_blocks[:, :, None] * BLOCK + offsets[None, None, :]).reshape(
        tile_count * 2 * BLOCK
    )
    chosen = jnp.take(phases, channels, axis=2)
    quarter = bins_local // win_count
    received = lax.all_to_all(chosen, "tile", split_axis=2, concat_axis=1, tiled=True)
    shaped = received.reshape(win_local, tile_count, win_count, quarter, 2 * BLOCK)
    arrived = lax.all_to_all(shaped, "win", split_axis=2, concat_axis=0, tiled=True)
    arrived = arrived.reshape(total_windows, tile_count * quarter, 2 * BLOCK)
    source_index = jnp.arange(tile_count, dtype=jnp.int32)[:, None]
    inner_index = jnp.arange(quarter, dtype=jnp.int32)[None, :]
    freq_index = (
        source_index * bins_local + lax.axis_index("win") * quarter + inner_index
    ).reshape(tile_count * quarter)
    cos_tab, sin_tab = tables_at(freq_index, total_bins, HALF, total_windows)
    cross_real, cross_imag = cross_spectra(arrived[:, :, :BLOCK], arrived[:, :, BLOCK:])
    partial_lags = to_lags(cross_real, cross_imag, cos_tab, sin_tab)
    lagged = lax.psum_scatter(partial_lags, "win", scatter_dimension=0, tiled=True)
    return lagged[None]


def on_device(phases, tile_blocks):
    tile_count = lax.axis_size("tile")
    windows, bins_local, _ = phases.shape
    lag_values = tile_count * BLOCK * BLOCK * (2 * HALF + 1)
    phase_values = tile_count * 2 * BLOCK * windows * bins_local
    fits = (
        lax.axis_size("win") == 4
        and tile_count * 2 * BLOCK == LANES
        and bins_local % (4 * LANES) == 0
        and windows % 4 == 0
        and phases.shape[2] % LANES == 0
    )
    if fits and lag_values < phase_values:
        return by_lags(phases, tile_blocks)
    return by_phases(phases, tile_blocks)


def solution(mesh):
    placed = (P(("groups", "win"), "tile", None), P())
    return jax.shard_map(
        on_device,
        mesh=mesh,
        in_specs=placed,
        out_specs=P(("groups", "tile"), "win", None, None),
        check_vma=False,
    )
```

```python
import functools
import math

import jax
import jax.numpy as jnp
import numpy as np
from jax import lax
from jax.experimental import pallas as pl
from jax.experimental.pallas import tpu as pltpu
from jax.sharding import PartitionSpec as P

BLOCK = 16
HALF = 256
LANES = 128
TAB_ROWS = 272
FRONT_VMEM = 50 * 2**20
LAG_VMEM = 50 * 2**20
LAG_ROWS = 264
SIN_FIT = (7.0710677816e-01, -2.9462767175e-02, 3.6827228729e-04, -2.1886110623e-06, 7.1958213082e-09)
COS_FIT = (1.4142134963e+00, -1.7677635964e-01, 3.6825748950e-03, -3.0612567514e-05, 1.2790438412e-07)


def lag_tables(total_bins, bins_local, windows):
    bins = np.arange(total_bins, dtype=np.int64)
    lags = np.arange(TAB_ROWS, dtype=np.int64)
    angles = np.mod(lags[:, None] * bins[None, :], 2 * total_bins) * (math.pi / total_bins)
    weight = np.where(bins == 0, 1.0, 2.0) / math.sqrt(2.0 * windows * total_bins)
    out = []
    for values in (weight * np.cos(angles), weight * np.sin(angles)):
        values = values.astype(np.float32)
        high = values.astype(jnp.bfloat16)
        low = (values - high.astype(np.float32)).astype(jnp.bfloat16)
        out.append(np.stack([high, low]))
    table = np.stack(out)
    table = table.reshape(2, 2, TAB_ROWS, total_bins // bins_local, bins_local)
    return np.ascontiguousarray(np.moveaxis(table, 3, 0))


def horner(coefs, z):
    acc = z * coefs[-1] + coefs[-2]
    for coef in coefs[-3::-1]:
        acc = acc * z + coef
    return acc


def sin_cos(x):
    z = x * x
    t = x * horner(SIN_FIT, z)
    q = horner(COS_FIT, z)
    return t * q, 1.0 - t * t


def front_kernel(tiles, ids_ref, phases_ref, tables_ref, out_ref, tab_ref, *refs):
    raw_ref, stage_ref, packed, turned = refs[0], refs[1], refs[2:4], refs[4:6]
    raw_sem, stage_sem, tab_sem = refs[6:]
    table_copy = pltpu.make_async_copy(tables_ref.at[ids_ref[0]], tab_ref, tab_sem)
    windows, bins_local, channels = raw_ref.shape
    units = bins_local // LANES
    per_lane_tile = LANES // BLOCK

    def raw_copy(unit):
        bins = pl.ds(unit * LANES, LANES)
        return pltpu.make_async_copy(phases_ref.at[:, bins, :], raw_ref.at[:, bins, :], raw_sem.at[unit])

    ahead = min(units, 4)
    for unit in range(ahead):
        raw_copy(unit).start()

    def stage_copy(unit):
        slot = unit % 2
        return pltpu.make_async_copy(stage_ref.at[slot], out_ref.at[:, unit], stage_sem.at[slot])

    lane = lax.broadcasted_iota(jnp.int32, (8, LANES), 1)
    at, col = lane % BLOCK, lane // BLOCK
    chip, core = ids_ref[1] // 2, ids_ref[1] % 2
    lead = ((at // 8) ^ core) * 4 + (((at // 4) % 2) ^ chip) * 8 + at % 4
    block = jnp.zeros_like(lane)
    for m in range(2 * tiles):
        block = jnp.where(col == m, ids_ref[2 + 2 * (ids_ref[0] ^ (m // 2)) + m % 2], block)
    row = jnp.where(col % 2 == 0, lead, at) + (block % per_lane_tile) * BLOCK
    row = jnp.tile(row, (BLOCK // 8, 1))
    source = jnp.tile(block // per_lane_tile, (BLOCK // 8, 1))

    def gather(item, to, piece):
        unit, w = item // windows, item % windows
        first = pl.multiple_of(unit * LANES + piece * BLOCK, BLOCK)
        value = None
        for q in range(channels // LANES):
            raw = raw_ref[w, pl.ds(first, BLOCK), q * LANES : (q + 1) * LANES]
            moved = jnp.take_along_axis(raw, row, axis=1)
            value = moved if value is None else jnp.where(source == q, moved, value)
        to[piece * BLOCK : (piece + 1) * BLOCK] = value

    def unfold(item, rows_ref, m):
        unit, w = item // windows, item % windows
        sin, cos = sin_cos(rows_ref[m * BLOCK : (m + 1) * BLOCK])
        stage_ref[unit % 2, m // 2, 0, w, m % 2] = cos
        stage_ref[unit % 2, m // 2, 1, w, m % 2] = sin

    pieces = range(LANES // BLOCK)
    raw_copy(0).wait()
    for piece in pieces:
        gather(0, packed[1], piece)
    turned[0][...] = packed[1][...].T
    for piece in pieces:
        gather(1, packed[0], piece)

    @pl.loop(0, units)
    def _(unit):
        @pl.when(unit + 1 < units)
        def _():
            raw_copy(unit + 1).wait()

        @pl.when(unit + ahead < units)
        def _():
            raw_copy(unit + ahead).start()

        @pl.when(unit == units // 2)
        def _():
            table_copy.start()

        @pl.when(unit >= 2)
        def _():
            stage_copy(unit - 2).wait()

        @pl.loop(0, windows // 4)
        def _(h):
            for j in range(4):
                item = unit * windows + 4 * h + j
                here, there = j % 2, 1 - j % 2
                turned[there][...] = packed[here][...].T
                for piece in pieces:
                    gather(jnp.minimum(item + 2, units * windows - 1), packed[there], piece)
                    unfold(item, turned[here], piece)

        stage_copy(unit).start()

    table_copy.wait()
    for unit in range(units - 2, units):
        stage_copy(unit).wait()


def waves_of(phases, ids, tables, tiles):
    windows, bins_local, channels = phases.shape
    table = jax.ShapeDtypeStruct(tables.shape[1:], tables.dtype)
    out = jax.ShapeDtypeStruct((tiles, bins_local // LANES, 2, windows, 2, BLOCK, LANES), jnp.float32)
    smem, vmem = pl.BlockSpec(memory_space=pltpu.SMEM), pl.BlockSpec(memory_space=pltpu.VMEM)
    return pl.pallas_call(
        functools.partial(front_kernel, tiles),
        in_specs=[smem] + [pl.BlockSpec(memory_space=pl.ANY)] * 2,
        out_specs=[pl.BlockSpec(memory_space=pl.ANY), vmem],
        out_shape=[out, table],
        scratch_shapes=[
            pltpu.VMEM(phases.shape, jnp.float32),
            pltpu.VMEM((2, tiles) + out.shape[2:], jnp.float32),
        ]
        + [pltpu.VMEM((LANES, LANES), jnp.float32)] * 4
        + [pltpu.SemaphoreType.DMA((k,)) for k in (bins_local // LANES, 2)]
        + [pltpu.SemaphoreType.DMA],
        compiler_params=pltpu.CompilerParams(vmem_limit_bytes=FRONT_VMEM),
        cost_estimate=pl.CostEstimate(flops=10**10, bytes_accessed=phases.size * 4, transcendentals=0),
        name="waves",
    )(ids, phases, tables)


def lag_kernel(m, after_ref, waves_ref, tab_ref, keep_ref, send_ref, wave_ref, plane_ref, spectra_ref, wave_sem):
    del after_ref
    units, _, windows = wave_ref.shape[:3]

    def wave_copy(unit):
        return pltpu.make_async_copy(waves_ref.at[m, unit], wave_ref.at[unit], wave_sem.at[unit])

    for unit in range(units):
        wave_copy(unit).start()

    @pl.loop(0, units)
    def _(unit):
        wave_copy(unit).wait()
        for w in range(windows):
            lead_cos, trail_cos = wave_ref[unit, 0, w, 0], wave_ref[unit, 0, w, 1]
            lead_sin, trail_sin = wave_ref[unit, 1, w, 0], wave_ref[unit, 1, w, 1]
            plane_ref[0, w, 0], plane_ref[1, w, 0], plane_ref[2, w, 0] = lead_cos + lead_sin, lead_sin, lead_cos
            plane_ref[0, w, 1], plane_ref[1, w, 1] = trail_cos, trail_cos - trail_sin
            plane_ref[2, w, 1] = trail_cos + trail_sin
        for quad in range(BLOCK // 4):
            sums = [[None] * 3 for _ in range(4)]
            for w in range(windows):
                for p in range(3):
                    right = plane_ref[p, w, 1]
                    for i in range(4):
                        row = quad * 4 + i
                        prod = plane_ref[p, w, 0, row : row + 1, :] * right
                        sums[i][p] = prod if w == 0 else sums[i][p] + prod
            for i in range(4):
                rows = slice((quad * 4 + i) * BLOCK, (quad * 4 + i + 1) * BLOCK)
                for part in range(2):
                    value = sums[i][0] - sums[i][1 + part]
                    high = value.astype(jnp.bfloat16)
                    low = value - high.astype(jnp.float32)
                    spectra_ref[unit, part, 0, rows] = high
                    spectra_ref[unit, part, 1, rows] = low.astype(jnp.bfloat16)

    def product(table, values):
        return lax.dot_general(
            table, values, (((1,), (1,)), ((), ())), preferred_element_type=jnp.float32
        )

    totals = []
    for part in range(2):
        high, low = (
            jnp.concatenate([spectra_ref[unit, part, half] for unit in range(units)], axis=1)
            for half in range(2)
        )
        tab_high, tab_low = tab_ref[part, 0], tab_ref[part, 1]
        totals.append(product(tab_high, high) + product(tab_low, high) + product(tab_high, low))
    middle = LANES // 2
    low_lanes = lax.broadcasted_iota(jnp.int32, (LAG_ROWS, LANES), 1) < middle
    for core, ref in enumerate((keep_ref, send_ref)):
        even, odd = (total[:LAG_ROWS, core * LANES : (core + 1) * LANES] for total in totals)
        ref[0] = jnp.where(low_lanes, even, pltpu.roll(odd, middle, 1))
        ref[1] = jnp.where(low_lanes, pltpu.roll(even, middle, 1), odd)


def partial_lags(m, waves, table, after):
    pairs = BLOCK * BLOCK
    planes = pltpu.VMEM((3,) + waves.shape[3:], jnp.float32)
    out = jax.ShapeDtypeStruct((2, LAG_ROWS, LANES), jnp.float32)
    vmem = pl.BlockSpec(memory_space=pltpu.VMEM)
    return pl.pallas_call(
        functools.partial(lag_kernel, m),
        in_specs=[pl.BlockSpec(memory_space=pltpu.SMEM), pl.BlockSpec(memory_space=pl.ANY), vmem],
        out_specs=[vmem, vmem],
        out_shape=[out, out],
        scratch_shapes=[
            pltpu.VMEM(waves.shape[1:], jnp.float32),
            planes,
            pltpu.VMEM((waves.shape[1], 2, 2, pairs, LANES), jnp.bfloat16),
            pltpu.SemaphoreType.DMA(waves.shape[1:2]),
        ],
        compiler_params=pltpu.CompilerParams(vmem_limit_bytes=LAG_VMEM),
        cost_estimate=pl.CostEstimate(flops=4 * 10**9, bytes_accessed=waves.size, transcendentals=0),
        name="partial_lags",
    )(after, waves, table)


def finish_kernel(*refs):
    out_ref = refs[-1]
    total = refs[0][...]
    for ref in refs[1:-1]:
        total = total + ref[...]
    half = LANES // 2
    other = pltpu.roll(total, half, 1)
    low_lanes = lax.broadcasted_iota(jnp.int32, total.shape, 1) < half
    both = jnp.where(low_lanes, total - other, total + other)
    rows, trailing = out_ref.shape[0], out_ref.shape[1]
    mirror = LANES - 1 - lax.broadcasted_iota(jnp.int32, (half, LANES), 1)
    for k in range(HALF // LANES):
        ahead = both[k * LANES : (k + 1) * LANES, :].T[:half]
        first = HALF + k * LANES
        out_ref[:, :, first : first + LANES] = ahead.reshape(rows, trailing, LANES)
        turned = both[k * LANES + 1 : (k + 1) * LANES + 1, :].T
        behind = jnp.take_along_axis(turned[half:], mirror, axis=1)
        first = HALF - (k + 1) * LANES
        out_ref[:, :, first : first + LANES] = behind.reshape(rows, trailing, LANES)
    last = turned[:half, LANES - 1 :]
    out_ref[:, :, 2 * HALF :] = last.reshape(rows, trailing, 1)


def finish(parts):
    rows = BLOCK // 4
    return pl.pallas_call(
        finish_kernel,
        out_shape=jax.ShapeDtypeStruct((rows, BLOCK, 2 * HALF + 1), jnp.float32),
        name="finish",
    )(*parts)


def by_lags(phases, tile_blocks):
    tile_count = lax.axis_size("tile")
    win_count = lax.axis_size("win")
    windows, bins_local, _ = phases.shape
    place = jnp.stack([lax.axis_index("tile"), lax.axis_index("win")])
    ids = jnp.concatenate([place, tile_blocks.reshape(-1)])
    tables = jnp.asarray(lag_tables(bins_local * tile_count, bins_local, windows * win_count))
    cross_core = [(w, w ^ 1) for w in range(win_count)]
    cross_chip = [(w, w ^ 2) for w in range(win_count)]
    waves, table = waves_of(phases, ids, tables, tile_count)
    after = ids[:1]
    keep, came, away, part = {}, {}, {}, {}

    def over_core(m):
        keep[m], send = partial_lags(m, waves, table, after)
        came[m] = lax.ppermute(send, "win", cross_core)

    def over_chip(m):
        part[m] = keep[m][0] + came[m][0] + lax.ppermute(away[m], "win", cross_chip)

    def over_tile(m):
        part[m] = lax.ppermute(part[m], "tile", [(z, z ^ m) for z in range(tile_count)])

    over_core(3)
    over_core(2)
    away[3] = keep[3][1] + came[3][1]
    after, away[3] = lax.optimization_barrier((after, away[3]))
    over_chip(3)
    over_core(1)
    away[2] = keep[2][1] + came[2][1]
    after, away[2], part[3] = lax.optimization_barrier((after, away[2], part[3]))
    over_chip(2)
    over_tile(3)
    over_core(0)
    over_tile(2)
    for m in (1, 0):
        away[m] = keep[m][1] + came[m][1]
        over_chip(m)
    over_tile(1)
    parts = [part[m] for m in (3, 2, 1, 0)]
    return finish(parts)[None]


def tables_at(freq_index, bin_count, half_lags, windows):
    freq_index = freq_index[:, None]
    lag_index = jnp.arange(2 * half_lags + 1, dtype=jnp.int32)[None, :] - half_lags
    phase_turns = jnp.mod(freq_index * lag_index, 2 * bin_count).astype(jnp.float32)
    angles = phase_turns * jnp.float32(math.pi / bin_count)
    weight = jnp.where(freq_index == 0, 1.0, 2.0).astype(jnp.float32) / jnp.float32(
        math.sqrt(2.0 * windows * bin_count)
    )
    return (weight * jnp.cos(angles), -weight * jnp.sin(angles))


def cross_spectra(leading, trailing):
    cos_lead, sin_lead = (jnp.cos(leading), jnp.sin(leading))
    cos_trail, sin_trail = (jnp.cos(trailing), jnp.sin(trailing))
    highest = lax.Precision.HIGHEST
    cross_real = jnp.einsum("wfi,wfj->fij", cos_lead, cos_trail, precision=highest) + jnp.einsum(
        "wfi,wfj->fij", sin_lead, sin_trail, precision=highest
    )
    cross_imag = jnp.einsum("wfi,wfj->fij", sin_lead, cos_trail, precision=highest) - jnp.einsum(
        "wfi,wfj->fij", cos_lead, sin_trail, precision=highest
    )
    return (cross_real, cross_imag)


def to_lags(cross_real, cross_imag, cos_tab, sin_tab):
    bin_count, rows_a, rows_b = cross_real.shape
    dims = (((0,), (0,)), ((), ()))
    highest = lax.Precision.HIGHEST
    lagged = lax.dot_general(
        cross_real.reshape(bin_count, rows_a * rows_b), cos_tab, dims, precision=highest
    )
    lagged = lagged + lax.dot_general(
        cross_imag.reshape(bin_count, rows_a * rows_b), sin_tab, dims, precision=highest
    )
    return lagged.reshape(rows_a, rows_b, cos_tab.shape[1])


def by_phases(phases, tile_blocks):
    tile_count = lax.axis_size("tile")
    win_count = lax.axis_size("win")
    win_local = phases.shape[0]
    bins_local = phases.shape[1]
    total_bins = bins_local * tile_count
    total_windows = win_local * win_count
    offsets = jnp.arange(BLOCK, dtype=jnp.int32)
    channels = (tile_blocks[:, :, None] * BLOCK + offsets[None, None, :]).reshape(
        tile_count * 2 * BLOCK
    )
    chosen = jnp.take(phases, channels, axis=2)
    quarter = bins_local // win_count
    received = lax.all_to_all(chosen, "tile", split_axis=2, concat_axis=1, tiled=True)
    shaped = received.reshape(win_local, tile_count, win_count, quarter, 2 * BLOCK)
    arrived = lax.all_to_all(shaped, "win", split_axis=2, concat_axis=0, tiled=True)
    arrived = arrived.reshape(total_windows, tile_count * quarter, 2 * BLOCK)
    source_index = jnp.arange(tile_count, dtype=jnp.int32)[:, None]
    inner_index = jnp.arange(quarter, dtype=jnp.int32)[None, :]
    freq_index = (
        source_index * bins_local + lax.axis_index("win") * quarter + inner_index
    ).reshape(tile_count * quarter)
    cos_tab, sin_tab = tables_at(freq_index, total_bins, HALF, total_windows)
    cross_real, cross_imag = cross_spectra(arrived[:, :, :BLOCK], arrived[:, :, BLOCK:])
    partial_lags = to_lags(cross_real, cross_imag, cos_tab, sin_tab)
    lagged = lax.psum_scatter(partial_lags, "win", scatter_dimension=0, tiled=True)
    return lagged[None]


def on_device(phases, tile_blocks):
    tile_count = lax.axis_size("tile")
    windows, bins_local, _ = phases.shape
    lag_values = tile_count * BLOCK * BLOCK * (2 * HALF + 1)
    phase_values = tile_count * 2 * BLOCK * windows * bins_local
    fits = (
        lax.axis_size("win") == 4
        and tile_count * 2 * BLOCK == LANES
        and bins_local % (4 * LANES) == 0
        and windows % 4 == 0
        and phases.shape[2] % LANES == 0
    )
    if fits and lag_values < phase_values:
        return by_lags(phases, tile_blocks)
    return by_phases(phases, tile_blocks)


def solution(mesh):
    placed = (P(("groups", "win"), "tile", None), P())
    return jax.shard_map(
        on_device,
        mesh=mesh,
        in_specs=placed,
        out_specs=P(("groups", "tile"), "win", None, None),
        check_vma=False,
    )
```

```python
import functools
import math

import jax
import jax.numpy as jnp
import numpy as np
from jax import lax
from jax.experimental import pallas as pl
from jax.experimental.pallas import tpu as pltpu
from jax.sharding import PartitionSpec as P

BLOCK = 16
HALF = 256
LANES = 128
TAB_ROWS = 272
FRONT_VMEM = 50 * 2**20
LAG_VMEM = 50 * 2**20
LAG_ROWS = 264
SIN_FIT = (7.0710677816e-01, -2.9462767175e-02, 3.6827228729e-04, -2.1886110623e-06, 7.1958213082e-09)
COS_FIT = (1.4142134963e+00, -1.7677635964e-01, 3.6825748950e-03, -3.0612567514e-05, 1.2790438412e-07)


def lag_tables(total_bins, bins_local, windows):
    bins = np.arange(total_bins, dtype=np.int64)
    lags = np.arange(TAB_ROWS, dtype=np.int64)
    angles = np.mod(lags[:, None] * bins[None, :], 2 * total_bins) * (math.pi / total_bins)
    weight = np.where(bins == 0, 1.0, 2.0) / math.sqrt(2.0 * windows * total_bins)
    out = []
    for values in (weight * np.cos(angles), weight * np.sin(angles)):
        values = values.astype(np.float32)
        high = values.astype(jnp.bfloat16)
        low = (values - high.astype(np.float32)).astype(jnp.bfloat16)
        out.append(np.stack([high, low]))
    table = np.stack(out)
    table = table.reshape(2, 2, TAB_ROWS, total_bins // bins_local, bins_local)
    return np.ascontiguousarray(np.moveaxis(table, 3, 0))


def horner(coefs, z):
    acc = z * coefs[-1] + coefs[-2]
    for coef in coefs[-3::-1]:
        acc = acc * z + coef
    return acc


def sin_cos(x):
    z = x * x
    t = x * horner(SIN_FIT, z)
    q = horner(COS_FIT, z)
    return t * q, 1.0 - t * t


def front_kernel(tiles, ids_ref, phases_ref, tables_ref, out_ref, tab_ref, *refs):
    raw_ref, stage_ref, packed, turned = refs[0], refs[1], refs[2:4], refs[4:6]
    raw_sem, stage_sem, tab_sem = refs[6:]
    table_copy = pltpu.make_async_copy(tables_ref.at[ids_ref[0]], tab_ref, tab_sem)
    windows, bins_local, channels = raw_ref.shape
    units = bins_local // LANES
    per_lane_tile = LANES // BLOCK

    def raw_copy(unit):
        bins = pl.ds(unit * LANES, LANES)
        return pltpu.make_async_copy(phases_ref.at[:, bins, :], raw_ref.at[:, bins, :], raw_sem.at[unit])

    ahead = min(units, 4)
    for unit in range(ahead):
        raw_copy(unit).start()

    def stage_copy(unit):
        slot = unit % 2
        return pltpu.make_async_copy(stage_ref.at[slot], out_ref.at[:, unit], stage_sem.at[slot])

    lane = lax.broadcasted_iota(jnp.int32, (8, LANES), 1)
    at, col = lane % BLOCK, lane // BLOCK
    chip, core = ids_ref[1] // 2, ids_ref[1] % 2
    lead = ((at // 8) ^ core) * 4 + (((at // 4) % 2) ^ chip) * 8 + at % 4
    block = jnp.zeros_like(lane)
    for m in range(2 * tiles):
        block = jnp.where(col == m, ids_ref[2 + 2 * (ids_ref[0] ^ (m // 2)) + m % 2], block)
    row = jnp.where(col % 2 == 0, lead, at) + (block % per_lane_tile) * BLOCK
    row = jnp.tile(row, (BLOCK // 8, 1))
    source = jnp.tile(block // per_lane_tile, (BLOCK // 8, 1))

    def gather(item, to, piece):
        unit, w = item // windows, item % windows
        first = pl.multiple_of(unit * LANES + piece * BLOCK, BLOCK)
        value = None
        for q in range(channels // LANES):
            raw = raw_ref[w, pl.ds(first, BLOCK), q * LANES : (q + 1) * LANES]
            moved = jnp.take_along_axis(raw, row, axis=1)
            value = moved if value is None else jnp.where(source == q, moved, value)
        to[piece * BLOCK : (piece + 1) * BLOCK] = value

    def unfold(item, rows_ref, m):
        unit, w = item // windows, item % windows
        sin, cos = sin_cos(rows_ref[m * BLOCK : (m + 1) * BLOCK])
        stage_ref[unit % 2, m // 2, 0, w, m % 2] = cos
        stage_ref[unit % 2, m // 2, 1, w, m % 2] = sin

    eye = lax.broadcasted_iota(jnp.int32, (LANES, LANES), 0) == lax.broadcasted_iota(jnp.int32, (LANES, LANES), 1)
    eye = eye.astype(jnp.float32).astype(jnp.bfloat16)

    def turn(value):
        total = None
        for _ in range(3):
            term = value.astype(jnp.bfloat16)
            value = value - term.astype(jnp.float32)
            part = lax.dot_general(eye, term, (((1,), (1,)), ((), ())), preferred_element_type=jnp.float32)
            total = part if total is None else total + part
        return total

    pieces = range(LANES // BLOCK)
    raw_copy(0).wait()
    for piece in pieces:
        gather(0, packed[1], piece)
    turned[0][...] = turn(packed[1][...])
    for piece in pieces:
        gather(1, packed[0], piece)

    @pl.loop(0, units)
    def _(unit):
        @pl.when(unit + 1 < units)
        def _():
            raw_copy(unit + 1).wait()

        @pl.when(unit + ahead < units)
        def _():
            raw_copy(unit + ahead).start()

        @pl.when(unit == units // 2)
        def _():
            table_copy.start()

        @pl.when(unit >= 2)
        def _():
            stage_copy(unit - 2).wait()

        @pl.loop(0, windows // 8)
        def _(h):
            for j in range(8):
                item = unit * windows + 8 * h + j
                here, there = j % 2, 1 - j % 2
                for piece in pieces:
                    unfold(item, turned[here], piece)
                    gather(jnp.minimum(item + 2, units * windows - 1), packed[there], piece)
                turned[there][...] = turn(packed[here][...])

        stage_copy(unit).start()

    table_copy.wait()
    for unit in range(units - 2, units):
        stage_copy(unit).wait()


def waves_of(phases, ids, tables, tiles):
    windows, bins_local, channels = phases.shape
    table = jax.ShapeDtypeStruct(tables.shape[1:], tables.dtype)
    out = jax.ShapeDtypeStruct((tiles, bins_local // LANES, 2, windows, 2, BLOCK, LANES), jnp.float32)
    smem, vmem = pl.BlockSpec(memory_space=pltpu.SMEM), pl.BlockSpec(memory_space=pltpu.VMEM)
    return pl.pallas_call(
        functools.partial(front_kernel, tiles),
        in_specs=[smem] + [pl.BlockSpec(memory_space=pl.ANY)] * 2,
        out_specs=[pl.BlockSpec(memory_space=pl.ANY), vmem],
        out_shape=[out, table],
        scratch_shapes=[
            pltpu.VMEM(phases.shape, jnp.float32),
            pltpu.VMEM((2, tiles) + out.shape[2:], jnp.float32),
        ]
        + [pltpu.VMEM((LANES, LANES), jnp.float32)] * 4
        + [pltpu.SemaphoreType.DMA((k,)) for k in (bins_local // LANES, 2)]
        + [pltpu.SemaphoreType.DMA],
        compiler_params=pltpu.CompilerParams(vmem_limit_bytes=FRONT_VMEM),
        cost_estimate=pl.CostEstimate(flops=10**10, bytes_accessed=phases.size * 4, transcendentals=0),
        name="waves",
    )(ids, phases, tables)


def lag_kernel(m, after_ref, waves_ref, tab_ref, keep_ref, send_ref, wave_ref, plane_ref, spectra_ref, wave_sem):
    del after_ref
    units, _, windows = wave_ref.shape[:3]

    def wave_copy(unit):
        return pltpu.make_async_copy(waves_ref.at[m, unit], wave_ref.at[unit], wave_sem.at[unit])

    for unit in range(units):
        wave_copy(unit).start()

    @pl.loop(0, units)
    def _(unit):
        wave_copy(unit).wait()
        for w in range(windows):
            lead_cos, trail_cos = wave_ref[unit, 0, w, 0], wave_ref[unit, 0, w, 1]
            lead_sin, trail_sin = wave_ref[unit, 1, w, 0], wave_ref[unit, 1, w, 1]
            plane_ref[0, w, 0], plane_ref[1, w, 0], plane_ref[2, w, 0] = lead_cos + lead_sin, lead_sin, lead_cos
            plane_ref[0, w, 1], plane_ref[1, w, 1] = trail_cos, trail_cos - trail_sin
            plane_ref[2, w, 1] = trail_cos + trail_sin
        for quad in range(BLOCK // 4):
            sums = [[None] * 3 for _ in range(4)]
            for w in range(windows):
                for p in range(3):
                    right = plane_ref[p, w, 1]
                    for i in range(4):
                        row = quad * 4 + i
                        prod = plane_ref[p, w, 0, row : row + 1, :] * right
                        sums[i][p] = prod if w == 0 else sums[i][p] + prod
            for i in range(4):
                rows = slice((quad * 4 + i) * BLOCK, (quad * 4 + i + 1) * BLOCK)
                for part in range(2):
                    value = sums[i][0] - sums[i][1 + part]
                    high = value.astype(jnp.bfloat16)
                    low = value - high.astype(jnp.float32)
                    spectra_ref[unit, part, 0, rows] = high
                    spectra_ref[unit, part, 1, rows] = low.astype(jnp.bfloat16)

    def product(table, values):
        return lax.dot_general(
            table, values, (((1,), (1,)), ((), ())), preferred_element_type=jnp.float32
        )

    totals = []
    for part in range(2):
        high, low = (
            jnp.concatenate([spectra_ref[unit, part, half] for unit in range(units)], axis=1)
            for half in range(2)
        )
        tab_high, tab_low = tab_ref[part, 0], tab_ref[part, 1]
        totals.append(product(tab_high, high) + product(tab_low, high) + product(tab_high, low))
    middle = LANES // 2
    low_lanes = lax.broadcasted_iota(jnp.int32, (LAG_ROWS, LANES), 1) < middle
    for core, ref in enumerate((keep_ref, send_ref)):
        even, odd = (total[:LAG_ROWS, core * LANES : (core + 1) * LANES] for total in totals)
        ref[0] = jnp.where(low_lanes, even, pltpu.roll(odd, middle, 1))
        ref[1] = jnp.where(low_lanes, pltpu.roll(even, middle, 1), odd)


def partial_lags(m, waves, table, after):
    pairs = BLOCK * BLOCK
    planes = pltpu.VMEM((3,) + waves.shape[3:], jnp.float32)
    out = jax.ShapeDtypeStruct((2, LAG_ROWS, LANES), jnp.float32)
    vmem = pl.BlockSpec(memory_space=pltpu.VMEM)
    return pl.pallas_call(
        functools.partial(lag_kernel, m),
        in_specs=[pl.BlockSpec(memory_space=pltpu.SMEM), pl.BlockSpec(memory_space=pl.ANY), vmem],
        out_specs=[vmem, vmem],
        out_shape=[out, out],
        scratch_shapes=[
            pltpu.VMEM(waves.shape[1:], jnp.float32),
            planes,
            pltpu.VMEM((waves.shape[1], 2, 2, pairs, LANES), jnp.bfloat16),
            pltpu.SemaphoreType.DMA(waves.shape[1:2]),
        ],
        compiler_params=pltpu.CompilerParams(vmem_limit_bytes=LAG_VMEM),
        cost_estimate=pl.CostEstimate(flops=4 * 10**9, bytes_accessed=waves.size, transcendentals=0),
        name="partial_lags",
    )(after, waves, table)


def finish_kernel(*refs):
    out_ref = refs[-1]
    total = refs[0][...]
    for ref in refs[1:-1]:
        total = total + ref[...]
    half = LANES // 2
    other = pltpu.roll(total, half, 1)
    low_lanes = lax.broadcasted_iota(jnp.int32, total.shape, 1) < half
    both = jnp.where(low_lanes, total - other, total + other)
    rows, trailing = out_ref.shape[0], out_ref.shape[1]
    mirror = LANES - 1 - lax.broadcasted_iota(jnp.int32, (half, LANES), 1)
    for k in range(HALF // LANES):
        ahead = both[k * LANES : (k + 1) * LANES, :].T[:half]
        first = HALF + k * LANES
        out_ref[:, :, first : first + LANES] = ahead.reshape(rows, trailing, LANES)
        turned = both[k * LANES + 1 : (k + 1) * LANES + 1, :].T
        behind = jnp.take_along_axis(turned[half:], mirror, axis=1)
        first = HALF - (k + 1) * LANES
        out_ref[:, :, first : first + LANES] = behind.reshape(rows, trailing, LANES)
    last = turned[:half, LANES - 1 :]
    out_ref[:, :, 2 * HALF :] = last.reshape(rows, trailing, 1)


def finish(parts):
    rows = BLOCK // 4
    return pl.pallas_call(
        finish_kernel,
        out_shape=jax.ShapeDtypeStruct((rows, BLOCK, 2 * HALF + 1), jnp.float32),
        name="finish",
    )(*parts)


def by_lags(phases, tile_blocks):
    tile_count = lax.axis_size("tile")
    win_count = lax.axis_size("win")
    windows, bins_local, _ = phases.shape
    place = jnp.stack([lax.axis_index("tile"), lax.axis_index("win")])
    ids = jnp.concatenate([place, tile_blocks.reshape(-1)])
    tables = jnp.asarray(lag_tables(bins_local * tile_count, bins_local, windows * win_count))
    cross_core = [(w, w ^ 1) for w in range(win_count)]
    cross_chip = [(w, w ^ 2) for w in range(win_count)]
    waves, table = waves_of(phases, ids, tables, tile_count)
    after = ids[:1]
    keep, came, away, part = {}, {}, {}, {}

    def over_core(m):
        keep[m], send = partial_lags(m, waves, table, after)
        came[m] = lax.ppermute(send, "win", cross_core)

    def over_chip(m):
        part[m] = keep[m][0] + came[m][0] + lax.ppermute(away[m], "win", cross_chip)

    def over_tile(m):
        part[m] = lax.ppermute(part[m], "tile", [(z, z ^ m) for z in range(tile_count)])

    over_core(3)
    over_core(2)
    away[3] = keep[3][1] + came[3][1]
    after, away[3] = lax.optimization_barrier((after, away[3]))
    over_chip(3)
    over_core(1)
    away[2] = keep[2][1] + came[2][1]
    after, away[2], part[3] = lax.optimization_barrier((after, away[2], part[3]))
    over_chip(2)
    over_tile(3)
    over_core(0)
    over_tile(2)
    for m in (1, 0):
        away[m] = keep[m][1] + came[m][1]
        over_chip(m)
    over_tile(1)
    parts = [part[m] for m in (3, 2, 1, 0)]
    return finish(parts)[None]


def tables_at(freq_index, bin_count, half_lags, windows):
    freq_index = freq_index[:, None]
    lag_index = jnp.arange(2 * half_lags + 1, dtype=jnp.int32)[None, :] - half_lags
    phase_turns = jnp.mod(freq_index * lag_index, 2 * bin_count).astype(jnp.float32)
    angles = phase_turns * jnp.float32(math.pi / bin_count)
    weight = jnp.where(freq_index == 0, 1.0, 2.0).astype(jnp.float32) / jnp.float32(
        math.sqrt(2.0 * windows * bin_count)
    )
    return (weight * jnp.cos(angles), -weight * jnp.sin(angles))


def cross_spectra(leading, trailing):
    cos_lead, sin_lead = (jnp.cos(leading), jnp.sin(leading))
    cos_trail, sin_trail = (jnp.cos(trailing), jnp.sin(trailing))
    highest = lax.Precision.HIGHEST
    cross_real = jnp.einsum("wfi,wfj->fij", cos_lead, cos_trail, precision=highest) + jnp.einsum(
        "wfi,wfj->fij", sin_lead, sin_trail, precision=highest
    )
    cross_imag = jnp.einsum("wfi,wfj->fij", sin_lead, cos_trail, precision=highest) - jnp.einsum(
        "wfi,wfj->fij", cos_lead, sin_trail, precision=highest
    )
    return (cross_real, cross_imag)


def to_lags(cross_real, cross_imag, cos_tab, sin_tab):
    bin_count, rows_a, rows_b = cross_real.shape
    dims = (((0,), (0,)), ((), ()))
    highest = lax.Precision.HIGHEST
    lagged = lax.dot_general(
        cross_real.reshape(bin_count, rows_a * rows_b), cos_tab, dims, precision=highest
    )
    lagged = lagged + lax.dot_general(
        cross_imag.reshape(bin_count, rows_a * rows_b), sin_tab, dims, precision=highest
    )
    return lagged.reshape(rows_a, rows_b, cos_tab.shape[1])


def by_phases(phases, tile_blocks):
    tile_count = lax.axis_size("tile")
    win_count = lax.axis_size("win")
    win_local = phases.shape[0]
    bins_local = phases.shape[1]
    total_bins = bins_local * tile_count
    total_windows = win_local * win_count
    offsets = jnp.arange(BLOCK, dtype=jnp.int32)
    channels = (tile_blocks[:, :, None] * BLOCK + offsets[None, None, :]).reshape(
        tile_count * 2 * BLOCK
    )
    chosen = jnp.take(phases, channels, axis=2)
    quarter = bins_local // win_count
    received = lax.all_to_all(chosen, "tile", split_axis=2, concat_axis=1, tiled=True)
    shaped = received.reshape(win_local, tile_count, win_count, quarter, 2 * BLOCK)
    arrived = lax.all_to_all(shaped, "win", split_axis=2, concat_axis=0, tiled=True)
    arrived = arrived.reshape(total_windows, tile_count * quarter, 2 * BLOCK)
    source_index = jnp.arange(tile_count, dtype=jnp.int32)[:, None]
    inner_index = jnp.arange(quarter, dtype=jnp.int32)[None, :]
    freq_index = (
        source_index * bins_local + lax.axis_index("win") * quarter + inner_index
    ).reshape(tile_count * quarter)
    cos_tab, sin_tab = tables_at(freq_index, total_bins, HALF, total_windows)
    cross_real, cross_imag = cross_spectra(arrived[:, :, :BLOCK], arrived[:, :, BLOCK:])
    partial_lags = to_lags(cross_real, cross_imag, cos_tab, sin_tab)
    lagged = lax.psum_scatter(partial_lags, "win", scatter_dimension=0, tiled=True)
    return lagged[None]


def on_device(phases, tile_blocks):
    tile_count = lax.axis_size("tile")
    windows, bins_local, _ = phases.shape
    lag_values = tile_count * BLOCK * BLOCK * (2 * HALF + 1)
    phase_values = tile_count * 2 * BLOCK * windows * bins_local
    fits = (
        lax.axis_size("win") == 4
        and tile_count * 2 * BLOCK == LANES
        and bins_local % (4 * LANES) == 0
        and windows % 4 == 0
        and phases.shape[2] % LANES == 0
    )
    if fits and lag_values < phase_values:
        return by_lags(phases, tile_blocks)
    return by_phases(phases, tile_blocks)


def solution(mesh):
    placed = (P(("groups", "win"), "tile", None), P())
    return jax.shard_map(
        on_device,
        mesh=mesh,
        in_specs=placed,
        out_specs=P(("groups", "tile"), "win", None, None),
        check_vma=False,
    )
```

```python
import functools
import math

import jax
import jax.numpy as jnp
import numpy as np
from jax import lax
from jax.experimental import pallas as pl
from jax.experimental.pallas import tpu as pltpu
from jax.sharding import PartitionSpec as P

BLOCK = 16
HALF = 256
LANES = 128
TAB_ROWS = 272
FRONT_VMEM = 50 * 2**20
LAG_VMEM = 50 * 2**20
LAG_ROWS = 264
SIN_FIT = (7.0710677816e-01, -2.9462767175e-02, 3.6827228729e-04, -2.1886110623e-06, 7.1958213082e-09)
COS_FIT = (1.4142134963e+00, -1.7677635964e-01, 3.6825748950e-03, -3.0612567514e-05, 1.2790438412e-07)


def lag_tables(total_bins, bins_local, windows):
    bins = np.arange(total_bins, dtype=np.int64)
    lags = np.arange(TAB_ROWS, dtype=np.int64)
    angles = np.mod(lags[:, None] * bins[None, :], 2 * total_bins) * (math.pi / total_bins)
    weight = np.where(bins == 0, 1.0, 2.0) / math.sqrt(2.0 * windows * total_bins)
    out = []
    for values in (weight * np.cos(angles), weight * np.sin(angles)):
        values = values.astype(np.float32)
        high = values.astype(jnp.bfloat16)
        low = (values - high.astype(np.float32)).astype(jnp.bfloat16)
        out.append(np.stack([high, low]))
    table = np.stack(out)
    table = table.reshape(2, 2, TAB_ROWS, total_bins // bins_local, bins_local)
    return np.ascontiguousarray(np.moveaxis(table, 3, 0))


def horner(coefs, z):
    acc = z * coefs[-1] + coefs[-2]
    for coef in coefs[-3::-1]:
        acc = acc * z + coef
    return acc


def sin_cos(x):
    z = x * x
    t = x * horner(SIN_FIT, z)
    q = horner(COS_FIT, z)
    return t * q, 1.0 - t * t


def front_kernel(tiles, blocks_ref, phases_ref, tables_ref, out_ref, tab_ref, *refs):
    raw_ref, stage_ref, packed, turned = refs[0], refs[1], refs[2:4], refs[4:6]
    held_ref, raw_sem, stage_sem, tab_sem, blocks_sem = refs[6:]
    place, me = lax.axis_index("tile"), lax.axis_index("win")
    table_copy = pltpu.make_async_copy(tables_ref.at[place], tab_ref, tab_sem)
    blocks_copy = pltpu.make_async_copy(blocks_ref, held_ref, blocks_sem)
    blocks_copy.start()
    windows, bins_local, channels = raw_ref.shape
    units = bins_local // LANES
    per_lane_tile = LANES // BLOCK

    def raw_copy(unit):
        bins = pl.ds(unit * LANES, LANES)
        return pltpu.make_async_copy(phases_ref.at[:, bins, :], raw_ref.at[:, bins, :], raw_sem.at[unit])

    ahead = min(units, 4)
    for unit in range(ahead):
        raw_copy(unit).start()

    def stage_copy(unit):
        slot = unit % 2
        return pltpu.make_async_copy(stage_ref.at[slot], out_ref.at[:, unit], stage_sem.at[slot])

    lane = lax.broadcasted_iota(jnp.int32, (8, LANES), 1)
    at, col = lane % BLOCK, lane // BLOCK
    chip, core = me // 2, me % 2
    blocks_copy.wait()
    lead = ((at // 8) ^ core) * 4 + (((at // 4) % 2) ^ chip) * 8 + at % 4
    block = jnp.zeros_like(lane)
    for t in range(tiles):
        for side in range(2):
            here = ((col // 2) ^ place == t) & (col % 2 == side)
            block = jnp.where(here, held_ref[t : t + 1, side : side + 1], block)
    row = jnp.where(col % 2 == 0, lead, at) + (block % per_lane_tile) * BLOCK
    row = jnp.tile(row, (BLOCK // 8, 1))
    source = jnp.tile(block // per_lane_tile, (BLOCK // 8, 1))

    def gather(item, to, piece):
        unit, w = item // windows, item % windows
        first = pl.multiple_of(unit * LANES + piece * BLOCK, BLOCK)
        value = None
        for q in range(channels // LANES):
            raw = raw_ref[w, pl.ds(first, BLOCK), q * LANES : (q + 1) * LANES]
            moved = jnp.take_along_axis(raw, row, axis=1)
            value = moved if value is None else jnp.where(source == q, moved, value)
        to[piece * BLOCK : (piece + 1) * BLOCK] = value

    def unfold(item, rows_ref, m):
        unit, w = item // windows, item % windows
        sin, cos = sin_cos(rows_ref[m * BLOCK : (m + 1) * BLOCK])
        stage_ref[unit % 2, m // 2, 0, w, m % 2] = cos
        stage_ref[unit % 2, m // 2, 1, w, m % 2] = sin

    eye = lax.broadcasted_iota(jnp.int32, (LANES, LANES), 0) == lax.broadcasted_iota(jnp.int32, (LANES, LANES), 1)
    eye = eye.astype(jnp.float32).astype(jnp.bfloat16)

    def turn(value):
        total = None
        for _ in range(3):
            term = value.astype(jnp.bfloat16)
            value = value - term.astype(jnp.float32)
            part = lax.dot_general(eye, term, (((1,), (1,)), ((), ())), preferred_element_type=jnp.float32)
            total = part if total is None else total + part
        return total

    pieces = range(LANES // BLOCK)
    raw_copy(0).wait()
    for piece in pieces:
        gather(0, packed[1], piece)
    turned[0][...] = turn(packed[1][...])
    for piece in pieces:
        gather(1, packed[0], piece)

    @pl.loop(0, units)
    def _(unit):
        @pl.when(unit + 1 < units)
        def _():
            raw_copy(unit + 1).wait()

        @pl.when(unit + ahead < units)
        def _():
            raw_copy(unit + ahead).start()

        @pl.when(unit == units // 2)
        def _():
            table_copy.start()

        @pl.when(unit >= 2)
        def _():
            stage_copy(unit - 2).wait()

        @pl.loop(0, windows // 8)
        def _(h):
            for j in range(8):
                item = unit * windows + 8 * h + j
                here, there = j % 2, 1 - j % 2
                for piece in pieces:
                    unfold(item, turned[here], piece)
                    gather(jnp.minimum(item + 2, units * windows - 1), packed[there], piece)
                turned[there][...] = turn(packed[here][...])

        stage_copy(unit).start()

    table_copy.wait()
    for unit in range(units - 2, units):
        stage_copy(unit).wait()


def waves_of(phases, tile_blocks, tables, tiles):
    windows, bins_local, channels = phases.shape
    table = jax.ShapeDtypeStruct(tables.shape[1:], tables.dtype)
    out = jax.ShapeDtypeStruct((tiles, bins_local // LANES, 2, windows, 2, BLOCK, LANES), jnp.float32)
    vmem = pl.BlockSpec(memory_space=pltpu.VMEM)
    return pl.pallas_call(
        functools.partial(front_kernel, tiles),
        in_specs=[pl.BlockSpec(memory_space=pl.ANY)] * 3,
        out_specs=[pl.BlockSpec(memory_space=pl.ANY), vmem],
        out_shape=[out, table],
        scratch_shapes=[
            pltpu.VMEM(phases.shape, jnp.float32),
            pltpu.VMEM((2, tiles) + out.shape[2:], jnp.float32),
        ]
        + [pltpu.VMEM((LANES, LANES), jnp.float32)] * 4
        + [pltpu.VMEM(tile_blocks.shape, jnp.int32)]
        + [pltpu.SemaphoreType.DMA((k,)) for k in (bins_local // LANES, 2)]
        + [pltpu.SemaphoreType.DMA] * 2,
        compiler_params=pltpu.CompilerParams(vmem_limit_bytes=FRONT_VMEM),
        cost_estimate=pl.CostEstimate(flops=10**10, bytes_accessed=phases.size * 4, transcendentals=0),
        name="waves",
    )(tile_blocks, phases, tables)


def lag_kernel(m, after_ref, waves_ref, tab_ref, keep_ref, send_ref, wave_ref, plane_ref, spectra_ref, wave_sem):
    del after_ref
    units, _, windows = wave_ref.shape[:3]

    def wave_copy(unit):
        return pltpu.make_async_copy(waves_ref.at[m, unit], wave_ref.at[unit], wave_sem.at[unit])

    for unit in range(units):
        wave_copy(unit).start()

    @pl.loop(0, units)
    def _(unit):
        wave_copy(unit).wait()
        for w in range(windows):
            lead_cos, trail_cos = wave_ref[unit, 0, w, 0], wave_ref[unit, 0, w, 1]
            lead_sin, trail_sin = wave_ref[unit, 1, w, 0], wave_ref[unit, 1, w, 1]
            plane_ref[0, w, 0], plane_ref[1, w, 0], plane_ref[2, w, 0] = lead_cos + lead_sin, lead_sin, lead_cos
            plane_ref[0, w, 1], plane_ref[1, w, 1] = trail_cos, trail_cos - trail_sin
            plane_ref[2, w, 1] = trail_cos + trail_sin
        for quad in range(BLOCK // 4):
            sums = [[None] * 3 for _ in range(4)]
            for w in range(windows):
                for p in range(3):
                    right = plane_ref[p, w, 1]
                    for i in range(4):
                        row = quad * 4 + i
                        prod = plane_ref[p, w, 0, row : row + 1, :] * right
                        sums[i][p] = prod if w == 0 else sums[i][p] + prod
            for i in range(4):
                rows = slice((quad * 4 + i) * BLOCK, (quad * 4 + i + 1) * BLOCK)
                for part in range(2):
                    value = sums[i][0] - sums[i][1 + part]
                    high = value.astype(jnp.bfloat16)
                    low = value - high.astype(jnp.float32)
                    spectra_ref[unit, part, 0, rows] = high
                    spectra_ref[unit, part, 1, rows] = low.astype(jnp.bfloat16)

    def product(table, values):
        return lax.dot_general(
            table, values, (((1,), (1,)), ((), ())), preferred_element_type=jnp.float32
        )

    totals = []
    for part in range(2):
        high, low = (
            jnp.concatenate([spectra_ref[unit, part, half] for unit in range(units)], axis=1)
            for half in range(2)
        )
        tab_high, tab_low = tab_ref[part, 0], tab_ref[part, 1]
        totals.append(product(tab_high, high) + product(tab_low, high) + product(tab_high, low))
    middle = LANES // 2
    low_lanes = lax.broadcasted_iota(jnp.int32, (LAG_ROWS, LANES), 1) < middle
    for core, ref in enumerate((keep_ref, send_ref)):
        even, odd = (total[:LAG_ROWS, core * LANES : (core + 1) * LANES] for total in totals)
        ref[0] = jnp.where(low_lanes, even, pltpu.roll(odd, middle, 1))
        ref[1] = jnp.where(low_lanes, pltpu.roll(even, middle, 1), odd)


def partial_lags(m, waves, table, after):
    pairs = BLOCK * BLOCK
    planes = pltpu.VMEM((3,) + waves.shape[3:], jnp.float32)
    out = jax.ShapeDtypeStruct((2, LAG_ROWS, LANES), jnp.float32)
    vmem = pl.BlockSpec(memory_space=pltpu.VMEM)
    return pl.pallas_call(
        functools.partial(lag_kernel, m),
        in_specs=[pl.BlockSpec(memory_space=pltpu.SMEM), pl.BlockSpec(memory_space=pl.ANY), vmem],
        out_specs=[vmem, vmem],
        out_shape=[out, out],
        scratch_shapes=[
            pltpu.VMEM(waves.shape[1:], jnp.float32),
            planes,
            pltpu.VMEM((waves.shape[1], 2, 2, pairs, LANES), jnp.bfloat16),
            pltpu.SemaphoreType.DMA(waves.shape[1:2]),
        ],
        compiler_params=pltpu.CompilerParams(vmem_limit_bytes=LAG_VMEM),
        cost_estimate=pl.CostEstimate(flops=4 * 10**9, bytes_accessed=waves.size, transcendentals=0),
        name="partial_lags",
    )(after, waves, table)


def finish_kernel(*refs):
    out_ref = refs[-1]
    total = refs[0][...]
    for ref in refs[1:-1]:
        total = total + ref[...]
    half = LANES // 2
    other = pltpu.roll(total, half, 1)
    low_lanes = lax.broadcasted_iota(jnp.int32, total.shape, 1) < half
    both = jnp.where(low_lanes, total - other, total + other)
    rows, trailing = out_ref.shape[0], out_ref.shape[1]
    mirror = LANES - 1 - lax.broadcasted_iota(jnp.int32, (half, LANES), 1)
    for k in range(HALF // LANES):
        ahead = both[k * LANES : (k + 1) * LANES, :].T[:half]
        first = HALF + k * LANES
        out_ref[:, :, first : first + LANES] = ahead.reshape(rows, trailing, LANES)
        turned = both[k * LANES + 1 : (k + 1) * LANES + 1, :].T
        behind = jnp.take_along_axis(turned[half:], mirror, axis=1)
        first = HALF - (k + 1) * LANES
        out_ref[:, :, first : first + LANES] = behind.reshape(rows, trailing, LANES)
    last = turned[:half, LANES - 1 :]
    out_ref[:, :, 2 * HALF :] = last.reshape(rows, trailing, 1)


def finish(parts):
    rows = BLOCK // 4
    return pl.pallas_call(
        finish_kernel,
        out_shape=jax.ShapeDtypeStruct((rows, BLOCK, 2 * HALF + 1), jnp.float32),
        name="finish",
    )(*parts)


def by_lags(phases, tile_blocks):
    tile_count = lax.axis_size("tile")
    win_count = lax.axis_size("win")
    windows, bins_local, _ = phases.shape
    tables = jnp.asarray(lag_tables(bins_local * tile_count, bins_local, windows * win_count))
    cross_core = [(w, w ^ 1) for w in range(win_count)]
    cross_chip = [(w, w ^ 2) for w in range(win_count)]
    waves, table = waves_of(phases, tile_blocks, tables, tile_count)
    after = jnp.zeros(1, jnp.int32)
    keep, came, away, part = {}, {}, {}, {}

    def over_core(m):
        keep[m], send = partial_lags(m, waves, table, after)
        came[m] = lax.ppermute(send, "win", cross_core)

    def over_chip(m):
        part[m] = keep[m][0] + came[m][0] + lax.ppermute(away[m], "win", cross_chip)

    def over_tile(m):
        part[m] = lax.ppermute(part[m], "tile", [(z, z ^ m) for z in range(tile_count)])

    over_core(3)
    over_core(2)
    away[3] = keep[3][1] + came[3][1]
    after, away[3] = lax.optimization_barrier((after, away[3]))
    over_chip(3)
    over_core(1)
    away[2] = keep[2][1] + came[2][1]
    after, away[2], part[3] = lax.optimization_barrier((after, away[2], part[3]))
    over_chip(2)
    over_tile(3)
    over_core(0)
    over_tile(2)
    for m in (1, 0):
        away[m] = keep[m][1] + came[m][1]
        over_chip(m)
    over_tile(1)
    parts = [part[m] for m in (3, 2, 1, 0)]
    return finish(parts)[None]


def tables_at(freq_index, bin_count, half_lags, windows):
    freq_index = freq_index[:, None]
    lag_index = jnp.arange(2 * half_lags + 1, dtype=jnp.int32)[None, :] - half_lags
    phase_turns = jnp.mod(freq_index * lag_index, 2 * bin_count).astype(jnp.float32)
    angles = phase_turns * jnp.float32(math.pi / bin_count)
    weight = jnp.where(freq_index == 0, 1.0, 2.0).astype(jnp.float32) / jnp.float32(
        math.sqrt(2.0 * windows * bin_count)
    )
    return (weight * jnp.cos(angles), -weight * jnp.sin(angles))


def cross_spectra(leading, trailing):
    cos_lead, sin_lead = (jnp.cos(leading), jnp.sin(leading))
    cos_trail, sin_trail = (jnp.cos(trailing), jnp.sin(trailing))
    highest = lax.Precision.HIGHEST
    cross_real = jnp.einsum("wfi,wfj->fij", cos_lead, cos_trail, precision=highest) + jnp.einsum(
        "wfi,wfj->fij", sin_lead, sin_trail, precision=highest
    )
    cross_imag = jnp.einsum("wfi,wfj->fij", sin_lead, cos_trail, precision=highest) - jnp.einsum(
        "wfi,wfj->fij", cos_lead, sin_trail, precision=highest
    )
    return (cross_real, cross_imag)


def to_lags(cross_real, cross_imag, cos_tab, sin_tab):
    bin_count, rows_a, rows_b = cross_real.shape
    dims = (((0,), (0,)), ((), ()))
    highest = lax.Precision.HIGHEST
    lagged = lax.dot_general(
        cross_real.reshape(bin_count, rows_a * rows_b), cos_tab, dims, precision=highest
    )
    lagged = lagged + lax.dot_general(
        cross_imag.reshape(bin_count, rows_a * rows_b), sin_tab, dims, precision=highest
    )
    return lagged.reshape(rows_a, rows_b, cos_tab.shape[1])


def by_phases(phases, tile_blocks):
    tile_count = lax.axis_size("tile")
    win_count = lax.axis_size("win")
    win_local = phases.shape[0]
    bins_local = phases.shape[1]
    total_bins = bins_local * tile_count
    total_windows = win_local * win_count
    offsets = jnp.arange(BLOCK, dtype=jnp.int32)
    channels = (tile_blocks[:, :, None] * BLOCK + offsets[None, None, :]).reshape(
        tile_count * 2 * BLOCK
    )
    chosen = jnp.take(phases, channels, axis=2)
    quarter = bins_local // win_count
    received = lax.all_to_all(chosen, "tile", split_axis=2, concat_axis=1, tiled=True)
    shaped = received.reshape(win_local, tile_count, win_count, quarter, 2 * BLOCK)
    arrived = lax.all_to_all(shaped, "win", split_axis=2, concat_axis=0, tiled=True)
    arrived = arrived.reshape(total_windows, tile_count * quarter, 2 * BLOCK)
    source_index = jnp.arange(tile_count, dtype=jnp.int32)[:, None]
    inner_index = jnp.arange(quarter, dtype=jnp.int32)[None, :]
    freq_index = (
        source_index * bins_local + lax.axis_index("win") * quarter + inner_index
    ).reshape(tile_count * quarter)
    cos_tab, sin_tab = tables_at(freq_index, total_bins, HALF, total_windows)
    cross_real, cross_imag = cross_spectra(arrived[:, :, :BLOCK], arrived[:, :, BLOCK:])
    partial_lags = to_lags(cross_real, cross_imag, cos_tab, sin_tab)
    lagged = lax.psum_scatter(partial_lags, "win", scatter_dimension=0, tiled=True)
    return lagged[None]


def on_device(phases, tile_blocks):
    tile_count = lax.axis_size("tile")
    windows, bins_local, _ = phases.shape
    lag_values = tile_count * BLOCK * BLOCK * (2 * HALF + 1)
    phase_values = tile_count * 2 * BLOCK * windows * bins_local
    fits = (
        lax.axis_size("win") == 4
        and tile_count * 2 * BLOCK == LANES
        and bins_local % (4 * LANES) == 0
        and windows % 4 == 0
        and phases.shape[2] % LANES == 0
    )
    if fits and lag_values < phase_values:
        return by_lags(phases, tile_blocks)
    return by_phases(phases, tile_blocks)


def solution(mesh):
    placed = (P(("groups", "win"), "tile", None), P())
    return jax.shard_map(
        on_device,
        mesh=mesh,
        in_specs=placed,
        out_specs=P(("groups", "tile"), "win", None, None),
        check_vma=False,
    )
```

```python
import functools
import math

import jax
import jax.numpy as jnp
import numpy as np
from jax import lax
from jax.experimental import pallas as pl
from jax.experimental.pallas import tpu as pltpu
from jax.sharding import PartitionSpec as P

BLOCK = 16
HALF = 256
LANES = 128
TAB_ROWS = 272
FRONT_VMEM = 50 * 2**20
LAG_VMEM = 50 * 2**20
LAG_ROWS = 264
SIN_FIT = (7.0710677816e-01, -2.9462767175e-02, 3.6827228729e-04, -2.1886110623e-06, 7.1958213082e-09)
COS_FIT = (1.4142134963e+00, -1.7677635964e-01, 3.6825748950e-03, -3.0612567514e-05, 1.2790438412e-07)


def lag_tables(total_bins, bins_local, windows):
    bins = np.arange(total_bins, dtype=np.int64)
    lags = np.arange(TAB_ROWS, dtype=np.int64)
    angles = np.mod(lags[:, None] * bins[None, :], 2 * total_bins) * (math.pi / total_bins)
    weight = np.where(bins == 0, 1.0, 2.0) / math.sqrt(2.0 * windows * total_bins)
    out = []
    for values in (weight * np.cos(angles), weight * np.sin(angles)):
        values = values.astype(np.float32)
        high = values.astype(jnp.bfloat16)
        low = (values - high.astype(np.float32)).astype(jnp.bfloat16)
        out.append(np.stack([high, low]))
    table = np.stack(out)
    table = table.reshape(2, 2, TAB_ROWS, total_bins // bins_local, bins_local)
    return np.ascontiguousarray(np.moveaxis(table, 3, 0))


def horner(coefs, z):
    acc = z * coefs[-1] + coefs[-2]
    for coef in coefs[-3::-1]:
        acc = acc * z + coef
    return acc


def sin_cos(x):
    z = x * x
    t = x * horner(SIN_FIT, z)
    q = horner(COS_FIT, z)
    return t * q, 1.0 - t * t


def front_kernel(tiles, blocks_ref, phases_ref, tables_ref, out_ref, tab_ref, *refs):
    raw_ref, stage_ref, packed, turned = refs[0], refs[1], refs[2:4], refs[4:6]
    held_ref, raw_sem, stage_sem, tab_sem, blocks_sem = refs[6:]
    place, me = lax.axis_index("tile"), lax.axis_index("win")
    table_copy = pltpu.make_async_copy(tables_ref.at[place], tab_ref, tab_sem)
    blocks_copy = pltpu.make_async_copy(blocks_ref, held_ref, blocks_sem)
    blocks_copy.start()
    windows, bins_local, channels = raw_ref.shape
    units = bins_local // LANES
    per_lane_tile = LANES // BLOCK

    def raw_copy(unit):
        bins = pl.ds(unit * LANES, LANES)
        return pltpu.make_async_copy(phases_ref.at[:, bins, :], raw_ref.at[:, bins, :], raw_sem.at[unit])

    ahead = min(units, 4)
    for unit in range(ahead):
        raw_copy(unit).start()

    def stage_copy(unit):
        slot = unit % 2
        return pltpu.make_async_copy(stage_ref.at[slot], out_ref.at[:, unit], stage_sem.at[slot])

    lane = lax.broadcasted_iota(jnp.int32, (8, LANES), 1)
    at, col = lane % BLOCK, lane // BLOCK
    core = me % 2
    blocks_copy.wait()
    lead = ((at // 8) ^ core) * 4 + ((at // 4) % 2) * 8 + at % 4
    block = jnp.zeros_like(lane)
    for t in range(tiles):
        for side in range(2):
            here = ((col // 2) ^ place == t) & (col % 2 == side)
            block = jnp.where(here, held_ref[t : t + 1, side : side + 1], block)
    row = jnp.where(col % 2 == 0, lead, at) + (block % per_lane_tile) * BLOCK
    row = jnp.tile(row, (BLOCK // 8, 1))
    source = jnp.tile(block // per_lane_tile, (BLOCK // 8, 1))

    def gather(item, to, piece):
        unit, w = item // windows, item % windows
        first = pl.multiple_of(unit * LANES + piece * BLOCK, BLOCK)
        value = None
        for q in range(channels // LANES):
            raw = raw_ref[w, pl.ds(first, BLOCK), q * LANES : (q + 1) * LANES]
            moved = jnp.take_along_axis(raw, row, axis=1)
            value = moved if value is None else jnp.where(source == q, moved, value)
        to[piece * BLOCK : (piece + 1) * BLOCK] = value

    def unfold(item, rows_ref, m):
        unit, w = item // windows, item % windows
        sin, cos = sin_cos(rows_ref[m * BLOCK : (m + 1) * BLOCK])
        stage_ref[unit % 2, m // 2, 0, w, m % 2] = cos
        stage_ref[unit % 2, m // 2, 1, w, m % 2] = sin

    eye = lax.broadcasted_iota(jnp.int32, (LANES, LANES), 0) == lax.broadcasted_iota(jnp.int32, (LANES, LANES), 1)
    eye = eye.astype(jnp.float32).astype(jnp.bfloat16)

    def turn(value):
        total = None
        for _ in range(3):
            term = value.astype(jnp.bfloat16)
            value = value - term.astype(jnp.float32)
            part = lax.dot_general(eye, term, (((1,), (1,)), ((), ())), preferred_element_type=jnp.float32)
            total = part if total is None else total + part
        return total

    pieces = range(LANES // BLOCK)
    raw_copy(0).wait()
    for piece in pieces:
        gather(0, packed[1], piece)
    turned[0][...] = turn(packed[1][...])
    for piece in pieces:
        gather(1, packed[0], piece)

    @pl.loop(0, units)
    def _(unit):
        @pl.when(unit + 1 < units)
        def _():
            raw_copy(unit + 1).wait()

        @pl.when(unit + ahead < units)
        def _():
            raw_copy(unit + ahead).start()

        @pl.when(unit == units // 2)
        def _():
            table_copy.start()

        @pl.when(unit >= 2)
        def _():
            stage_copy(unit - 2).wait()

        @pl.loop(0, windows // 8)
        def _(h):
            for j in range(8):
                item = unit * windows + 8 * h + j
                here, there = j % 2, 1 - j % 2
                for piece in pieces:
                    unfold(item, turned[here], piece)
                    gather(jnp.minimum(item + 2, units * windows - 1), packed[there], piece)
                turned[there][...] = turn(packed[here][...])

        stage_copy(unit).start()

    table_copy.wait()
    for unit in range(units - 2, units):
        stage_copy(unit).wait()


def waves_of(phases, tile_blocks, tables, tiles):
    windows, bins_local, channels = phases.shape
    table = jax.ShapeDtypeStruct(tables.shape[1:], tables.dtype)
    out = jax.ShapeDtypeStruct((tiles, bins_local // LANES, 2, windows, 2, BLOCK, LANES), jnp.float32)
    vmem = pl.BlockSpec(memory_space=pltpu.VMEM)
    return pl.pallas_call(
        functools.partial(front_kernel, tiles),
        in_specs=[pl.BlockSpec(memory_space=pl.ANY)] * 3,
        out_specs=[pl.BlockSpec(memory_space=pl.ANY), vmem],
        out_shape=[out, table],
        scratch_shapes=[
            pltpu.VMEM(phases.shape, jnp.float32),
            pltpu.VMEM((2, tiles) + out.shape[2:], jnp.float32),
        ]
        + [pltpu.VMEM((LANES, LANES), jnp.float32)] * 4
        + [pltpu.VMEM(tile_blocks.shape, jnp.int32)]
        + [pltpu.SemaphoreType.DMA((k,)) for k in (bins_local // LANES, 2)]
        + [pltpu.SemaphoreType.DMA] * 2,
        compiler_params=pltpu.CompilerParams(vmem_limit_bytes=FRONT_VMEM),
        cost_estimate=pl.CostEstimate(flops=10**10, bytes_accessed=phases.size * 4, transcendentals=0),
        name="waves",
    )(tile_blocks, phases, tables)


def lag_kernel(m, after_ref, waves_ref, tab_ref, keep_ref, send_ref, wave_ref, plane_ref, spectra_ref, wave_sem):
    del after_ref
    units, _, windows = wave_ref.shape[:3]

    def wave_copy(unit):
        return pltpu.make_async_copy(waves_ref.at[m, unit], wave_ref.at[unit], wave_sem.at[unit])

    for unit in range(units):
        wave_copy(unit).start()

    @pl.loop(0, units)
    def _(unit):
        wave_copy(unit).wait()
        for w in range(windows):
            lead_cos, trail_cos = wave_ref[unit, 0, w, 0], wave_ref[unit, 0, w, 1]
            lead_sin, trail_sin = wave_ref[unit, 1, w, 0], wave_ref[unit, 1, w, 1]
            plane_ref[0, w, 0], plane_ref[1, w, 0], plane_ref[2, w, 0] = lead_cos + lead_sin, lead_sin, lead_cos
            plane_ref[0, w, 1], plane_ref[1, w, 1] = trail_cos, trail_cos - trail_sin
            plane_ref[2, w, 1] = trail_cos + trail_sin
        for quad in range(BLOCK // 4):
            sums = [[None] * 3 for _ in range(4)]
            for w in range(windows):
                for p in range(3):
                    right = plane_ref[p, w, 1]
                    for i in range(4):
                        row = quad * 4 + i
                        prod = plane_ref[p, w, 0, row : row + 1, :] * right
                        sums[i][p] = prod if w == 0 else sums[i][p] + prod
            for i in range(4):
                for part in range(2):
                    first = ((quad ^ part) * 4 + i) * BLOCK
                    rows = slice(first, first + BLOCK)
                    value = sums[i][0] - sums[i][1 + part]
                    high = value.astype(jnp.bfloat16)
                    low = value - high.astype(jnp.float32)
                    spectra_ref[unit, part, 0, rows] = high
                    spectra_ref[unit, part, 1, rows] = low.astype(jnp.bfloat16)

    def product(table, values):
        return lax.dot_general(
            table, values, (((1,), (1,)), ((), ())), preferred_element_type=jnp.float32
        )

    totals = []
    for part in range(2):
        high, low = (
            jnp.concatenate([spectra_ref[unit, part, half] for unit in range(units)], axis=1)
            for half in range(2)
        )
        tab_high, tab_low = tab_ref[part, 0], tab_ref[part, 1]
        totals.append(product(tab_high, high) + product(tab_low, high) + product(tab_high, low))
    middle = LANES // 2
    chip = lax.axis_index("win") // 2
    low_lanes = lax.broadcasted_iota(jnp.int32, (LAG_ROWS, LANES), 1) < middle
    for core, ref in enumerate((keep_ref, send_ref)):
        even, odd = (total[:LAG_ROWS, core * LANES : (core + 1) * LANES] for total in totals)
        ref[chip] = jnp.where(low_lanes, even, odd)
        ref[1 - chip] = jnp.where(low_lanes, odd, even)


def partial_lags(m, waves, table, after):
    pairs = BLOCK * BLOCK
    planes = pltpu.VMEM((3,) + waves.shape[3:], jnp.float32)
    out = jax.ShapeDtypeStruct((2, LAG_ROWS, LANES), jnp.float32)
    vmem = pl.BlockSpec(memory_space=pltpu.VMEM)
    return pl.pallas_call(
        functools.partial(lag_kernel, m),
        in_specs=[pl.BlockSpec(memory_space=pltpu.SMEM), pl.BlockSpec(memory_space=pl.ANY), vmem],
        out_specs=[vmem, vmem],
        out_shape=[out, out],
        scratch_shapes=[
            pltpu.VMEM(waves.shape[1:], jnp.float32),
            planes,
            pltpu.VMEM((waves.shape[1], 2, 2, pairs, LANES), jnp.bfloat16),
            pltpu.SemaphoreType.DMA(waves.shape[1:2]),
        ],
        compiler_params=pltpu.CompilerParams(vmem_limit_bytes=LAG_VMEM),
        cost_estimate=pl.CostEstimate(flops=4 * 10**9, bytes_accessed=waves.size, transcendentals=0),
        name="partial_lags",
    )(after, waves, table)


def finish_kernel(*refs):
    out_ref = refs[-1]
    total = refs[0][...]
    for ref in refs[1:-1]:
        total = total + ref[...]
    half = LANES // 2
    other = pltpu.roll(total, half, 1)
    low_lanes = lax.broadcasted_iota(jnp.int32, total.shape, 1) < half
    sign = 1.0 - 2.0 * (lax.axis_index("win") // 2).astype(jnp.float32)
    both = jnp.where(low_lanes, sign * (total - other), total + other)
    rows, trailing = out_ref.shape[0], out_ref.shape[1]
    mirror = LANES - 1 - lax.broadcasted_iota(jnp.int32, (half, LANES), 1)
    for k in range(HALF // LANES):
        ahead = both[k * LANES : (k + 1) * LANES, :].T[:half]
        first = HALF + k * LANES
        out_ref[:, :, first : first + LANES] = ahead.reshape(rows, trailing, LANES)
        turned = both[k * LANES + 1 : (k + 1) * LANES + 1, :].T
        behind = jnp.take_along_axis(turned[half:], mirror, axis=1)
        first = HALF - (k + 1) * LANES
        out_ref[:, :, first : first + LANES] = behind.reshape(rows, trailing, LANES)
    last = turned[:half, LANES - 1 :]
    out_ref[:, :, 2 * HALF :] = last.reshape(rows, trailing, 1)


def finish(parts):
    rows = BLOCK // 4
    return pl.pallas_call(
        finish_kernel,
        out_shape=jax.ShapeDtypeStruct((rows, BLOCK, 2 * HALF + 1), jnp.float32),
        name="finish",
    )(*parts)


def by_lags(phases, tile_blocks):
    tile_count = lax.axis_size("tile")
    win_count = lax.axis_size("win")
    windows, bins_local, _ = phases.shape
    tables = jnp.asarray(lag_tables(bins_local * tile_count, bins_local, windows * win_count))
    cross_core = [(w, w ^ 1) for w in range(win_count)]
    cross_chip = [(w, w ^ 2) for w in range(win_count)]
    waves, table = waves_of(phases, tile_blocks, tables, tile_count)
    after = jnp.zeros(1, jnp.int32)
    keep, came, away, part = {}, {}, {}, {}

    def over_core(m):
        keep[m], send = partial_lags(m, waves, table, after)
        came[m] = lax.ppermute(send, "win", cross_core)

    def over_chip(m):
        part[m] = keep[m][0] + came[m][0] + lax.ppermute(away[m], "win", cross_chip)

    def over_tile(m):
        part[m] = lax.ppermute(part[m], "tile", [(z, z ^ m) for z in range(tile_count)])

    over_core(3)
    over_core(2)
    away[3] = keep[3][1] + came[3][1]
    after, away[3] = lax.optimization_barrier((after, away[3]))
    over_chip(3)
    over_core(1)
    away[2] = keep[2][1] + came[2][1]
    after, away[2], part[3] = lax.optimization_barrier((after, away[2], part[3]))
    over_chip(2)
    over_tile(3)
    over_core(0)
    over_tile(2)
    for m in (1, 0):
        away[m] = keep[m][1] + came[m][1]
        over_chip(m)
    over_tile(1)
    parts = [part[m] for m in (3, 2, 1, 0)]
    return finish(parts)[None]


def tables_at(freq_index, bin_count, half_lags, windows):
    freq_index = freq_index[:, None]
    lag_index = jnp.arange(2 * half_lags + 1, dtype=jnp.int32)[None, :] - half_lags
    phase_turns = jnp.mod(freq_index * lag_index, 2 * bin_count).astype(jnp.float32)
    angles = phase_turns * jnp.float32(math.pi / bin_count)
    weight = jnp.where(freq_index == 0, 1.0, 2.0).astype(jnp.float32) / jnp.float32(
        math.sqrt(2.0 * windows * bin_count)
    )
    return (weight * jnp.cos(angles), -weight * jnp.sin(angles))


def cross_spectra(leading, trailing):
    cos_lead, sin_lead = (jnp.cos(leading), jnp.sin(leading))
    cos_trail, sin_trail = (jnp.cos(trailing), jnp.sin(trailing))
    highest = lax.Precision.HIGHEST
    cross_real = jnp.einsum("wfi,wfj->fij", cos_lead, cos_trail, precision=highest) + jnp.einsum(
        "wfi,wfj->fij", sin_lead, sin_trail, precision=highest
    )
    cross_imag = jnp.einsum("wfi,wfj->fij", sin_lead, cos_trail, precision=highest) - jnp.einsum(
        "wfi,wfj->fij", cos_lead, sin_trail, precision=highest
    )
    return (cross_real, cross_imag)


def to_lags(cross_real, cross_imag, cos_tab, sin_tab):
    bin_count, rows_a, rows_b = cross_real.shape
    dims = (((0,), (0,)), ((), ()))
    highest = lax.Precision.HIGHEST
    lagged = lax.dot_general(
        cross_real.reshape(bin_count, rows_a * rows_b), cos_tab, dims, precision=highest
    )
    lagged = lagged + lax.dot_general(
        cross_imag.reshape(bin_count, rows_a * rows_b), sin_tab, dims, precision=highest
    )
    return lagged.reshape(rows_a, rows_b, cos_tab.shape[1])


def by_phases(phases, tile_blocks):
    tile_count = lax.axis_size("tile")
    win_count = lax.axis_size("win")
    win_local = phases.shape[0]
    bins_local = phases.shape[1]
    total_bins = bins_local * tile_count
    total_windows = win_local * win_count
    offsets = jnp.arange(BLOCK, dtype=jnp.int32)
    channels = (tile_blocks[:, :, None] * BLOCK + offsets[None, None, :]).reshape(
        tile_count * 2 * BLOCK
    )
    chosen = jnp.take(phases, channels, axis=2)
    quarter = bins_local // win_count
    received = lax.all_to_all(chosen, "tile", split_axis=2, concat_axis=1, tiled=True)
    shaped = received.reshape(win_local, tile_count, win_count, quarter, 2 * BLOCK)
    arrived = lax.all_to_all(shaped, "win", split_axis=2, concat_axis=0, tiled=True)
    arrived = arrived.reshape(total_windows, tile_count * quarter, 2 * BLOCK)
    source_index = jnp.arange(tile_count, dtype=jnp.int32)[:, None]
    inner_index = jnp.arange(quarter, dtype=jnp.int32)[None, :]
    freq_index = (
        source_index * bins_local + lax.axis_index("win") * quarter + inner_index
    ).reshape(tile_count * quarter)
    cos_tab, sin_tab = tables_at(freq_index, total_bins, HALF, total_windows)
    cross_real, cross_imag = cross_spectra(arrived[:, :, :BLOCK], arrived[:, :, BLOCK:])
    partial_lags = to_lags(cross_real, cross_imag, cos_tab, sin_tab)
    lagged = lax.psum_scatter(partial_lags, "win", scatter_dimension=0, tiled=True)
    return lagged[None]


def on_device(phases, tile_blocks):
    tile_count = lax.axis_size("tile")
    windows, bins_local, _ = phases.shape
    lag_values = tile_count * BLOCK * BLOCK * (2 * HALF + 1)
    phase_values = tile_count * 2 * BLOCK * windows * bins_local
    fits = (
        lax.axis_size("win") == 4
        and tile_count * 2 * BLOCK == LANES
        and bins_local % (4 * LANES) == 0
        and windows % 4 == 0
        and phases.shape[2] % LANES == 0
    )
    if fits and lag_values < phase_values:
        return by_lags(phases, tile_blocks)
    return by_phases(phases, tile_blocks)


def solution(mesh):
    placed = (P(("groups", "win"), "tile", None), P())
    return jax.shard_map(
        on_device,
        mesh=mesh,
        in_specs=placed,
        out_specs=P(("groups", "tile"), "win", None, None),
        check_vma=False,
    )
```

```python
import functools
import math

import jax
import jax.numpy as jnp
import numpy as np
from jax import lax
from jax.experimental import pallas as pl
from jax.experimental.pallas import tpu as pltpu
from jax.sharding import PartitionSpec as P

BLOCK = 16
HALF = 256
LANES = 128
TAB_ROWS = 272
FRONT_VMEM = 50 * 2**20
LAG_VMEM = 50 * 2**20
LAG_ROWS = 264
SIN_FIT = (7.0710677816e-01, -2.9462767175e-02, 3.6827228729e-04, -2.1886110623e-06, 7.1958213082e-09)
COS_FIT = (1.4142134963e+00, -1.7677635964e-01, 3.6825748950e-03, -3.0612567514e-05, 1.2790438412e-07)


def lag_tables(total_bins, bins_local, windows):
    bins = np.arange(total_bins, dtype=np.int64)
    lags = np.arange(TAB_ROWS, dtype=np.int64)
    angles = np.mod(lags[:, None] * bins[None, :], 2 * total_bins) * (math.pi / total_bins)
    weight = np.where(bins == 0, 1.0, 2.0) / math.sqrt(2.0 * windows * total_bins)
    out = []
    for values in (weight * np.cos(angles), weight * np.sin(angles)):
        values = values.astype(np.float32)
        high = values.astype(jnp.bfloat16)
        low = (values - high.astype(np.float32)).astype(jnp.bfloat16)
        out.append(np.stack([high, low]))
    table = np.stack(out)
    table = table.reshape(2, 2, TAB_ROWS, total_bins // bins_local, bins_local)
    return np.ascontiguousarray(np.moveaxis(table, 3, 0))


def horner(coefs, z):
    acc = z * coefs[-1] + coefs[-2]
    for coef in coefs[-3::-1]:
        acc = acc * z + coef
    return acc


def sin_cos(x):
    z = x * x
    t = x * horner(SIN_FIT, z)
    q = horner(COS_FIT, z)
    return t * q, 1.0 - t * t


def front_kernel(tiles, blocks_ref, phases_ref, tables_ref, out_ref, tab_ref, *refs):
    raw_ref, stage_ref, packed, turned = refs[0], refs[1], refs[2:4], refs[4:6]
    held_ref, raw_sem, stage_sem, tab_sem, blocks_sem = refs[6:]
    place, me = lax.axis_index("tile"), lax.axis_index("win")
    table_copy = pltpu.make_async_copy(tables_ref.at[place], tab_ref, tab_sem)
    blocks_copy = pltpu.make_async_copy(blocks_ref, held_ref, blocks_sem)
    blocks_copy.start()
    windows, bins_local, channels = raw_ref.shape
    units = bins_local // LANES
    per_lane_tile = LANES // BLOCK

    def raw_copy(unit):
        bins = pl.ds(unit * LANES, LANES)
        return pltpu.make_async_copy(phases_ref.at[:, bins, :], raw_ref.at[:, bins, :], raw_sem.at[unit])

    ahead = units
    for unit in range(ahead):
        raw_copy(unit).start()

    def stage_copy(unit):
        slot = unit % 2
        return pltpu.make_async_copy(stage_ref.at[slot], out_ref.at[:, unit], stage_sem.at[slot])

    lane = lax.broadcasted_iota(jnp.int32, (8, LANES), 1)
    at, col = lane % BLOCK, lane // BLOCK
    core = me % 2
    blocks_copy.wait()
    lead = ((at // 8) ^ core) * 4 + ((at // 4) % 2) * 8 + at % 4
    block = jnp.zeros_like(lane)
    for t in range(tiles):
        for side in range(2):
            here = ((col // 2) ^ place == t) & (col % 2 == side)
            block = jnp.where(here, held_ref[t : t + 1, side : side + 1], block)
    row = jnp.where(col % 2 == 0, lead, at) + (block % per_lane_tile) * BLOCK
    source = block // per_lane_tile

    def gather(item, to, piece):
        unit, w = item // windows, item % windows
        for first in range(piece * BLOCK, (piece + 1) * BLOCK, 8):
            bins = pl.ds(pl.multiple_of(unit * LANES + first, 8), 8)
            value = None
            for q in range(channels // LANES):
                moved = jnp.take_along_axis(raw_ref[w, bins, q * LANES : (q + 1) * LANES], row, axis=1)
                value = moved if value is None else jnp.where(source == q, moved, value)
            to[first : first + 8] = value

    def unfold(item, rows_ref, m):
        unit, w = item // windows, item % windows
        sin, cos = sin_cos(rows_ref[m * BLOCK : (m + 1) * BLOCK])
        stage_ref[unit % 2, m // 2, 0, w, m % 2] = cos
        stage_ref[unit % 2, m // 2, 1, w, m % 2] = sin

    eye = lax.broadcasted_iota(jnp.int32, (LANES, LANES), 0) == lax.broadcasted_iota(jnp.int32, (LANES, LANES), 1)
    eye = eye.astype(jnp.float32).astype(jnp.bfloat16)

    def turn(value):
        total = None
        for _ in range(3):
            term = value.astype(jnp.bfloat16)
            value = value - term.astype(jnp.float32)
            part = lax.dot_general(eye, term, (((1,), (1,)), ((), ())), preferred_element_type=jnp.float32)
            total = part if total is None else total + part
        return total

    pieces = range(LANES // BLOCK)
    raw_copy(0).wait()
    for piece in pieces:
        gather(0, packed[1], piece)
    turned[0][...] = turn(packed[1][...])
    for piece in pieces:
        gather(1, packed[0], piece)

    @pl.loop(0, units)
    def _(unit):
        @pl.when(unit + 1 < units)
        def _():
            raw_copy(unit + 1).wait()

        @pl.when(unit + ahead < units)
        def _():
            raw_copy(unit + ahead).start()

        @pl.when(unit == units // 2)
        def _():
            table_copy.start()

        @pl.when(unit >= 2)
        def _():
            stage_copy(unit - 2).wait()

        @pl.loop(0, windows // 8)
        def _(h):
            for j in range(8):
                item = unit * windows + 8 * h + j
                here, there = j % 2, 1 - j % 2
                for piece in pieces:
                    unfold(item, turned[here], piece)
                    gather(jnp.minimum(item + 2, units * windows - 1), packed[there], piece)
                turned[there][...] = turn(packed[here][...])

        stage_copy(unit).start()

    table_copy.wait()
    for unit in range(units - 2, units):
        stage_copy(unit).wait()


def waves_of(phases, tile_blocks, tables, tiles):
    windows, bins_local, channels = phases.shape
    table = jax.ShapeDtypeStruct(tables.shape[1:], tables.dtype)
    out = jax.ShapeDtypeStruct((tiles, bins_local // LANES, 2, windows, 2, BLOCK, LANES), jnp.float32)
    vmem = pl.BlockSpec(memory_space=pltpu.VMEM)
    return pl.pallas_call(
        functools.partial(front_kernel, tiles),
        in_specs=[pl.BlockSpec(memory_space=pl.ANY)] * 3,
        out_specs=[pl.BlockSpec(memory_space=pl.ANY), vmem],
        out_shape=[out, table],
        scratch_shapes=[
            pltpu.VMEM(phases.shape, jnp.float32),
            pltpu.VMEM((2, tiles) + out.shape[2:], jnp.float32),
        ]
        + [pltpu.VMEM((LANES, LANES), jnp.float32)] * 4
        + [pltpu.VMEM(tile_blocks.shape, jnp.int32)]
        + [pltpu.SemaphoreType.DMA((k,)) for k in (bins_local // LANES, 2)]
        + [pltpu.SemaphoreType.DMA] * 2,
        compiler_params=pltpu.CompilerParams(vmem_limit_bytes=FRONT_VMEM),
        cost_estimate=pl.CostEstimate(flops=10**10, bytes_accessed=phases.size * 4, transcendentals=0),
        name="waves",
    )(tile_blocks, phases, tables)


def lag_kernel(m, after_ref, waves_ref, tab_ref, keep_ref, send_ref, wave_ref, plane_ref, spectra_ref, wave_sem):
    del after_ref
    units, _, windows = wave_ref.shape[:3]

    def wave_copy(unit):
        return pltpu.make_async_copy(waves_ref.at[m, unit], wave_ref.at[unit], wave_sem.at[unit])

    for unit in range(units):
        wave_copy(unit).start()

    @pl.loop(0, units)
    def _(unit):
        wave_copy(unit).wait()
        for w in range(windows):
            lead_cos, trail_cos = wave_ref[unit, 0, w, 0], wave_ref[unit, 0, w, 1]
            lead_sin, trail_sin = wave_ref[unit, 1, w, 0], wave_ref[unit, 1, w, 1]
            plane_ref[0, w, 0], plane_ref[1, w, 0], plane_ref[2, w, 0] = lead_cos + lead_sin, lead_sin, lead_cos
            plane_ref[0, w, 1], plane_ref[1, w, 1] = trail_cos, trail_cos - trail_sin
            plane_ref[2, w, 1] = trail_cos + trail_sin
        for quad in range(BLOCK // 4):
            sums = [[None] * 3 for _ in range(4)]
            for w in range(windows):
                for p in range(3):
                    right = plane_ref[p, w, 1]
                    for i in range(4):
                        row = quad * 4 + i
                        prod = plane_ref[p, w, 0, row : row + 1, :] * right
                        sums[i][p] = prod if w == 0 else sums[i][p] + prod
            for i in range(4):
                for part in range(2):
                    first = ((quad ^ part) * 4 + i) * BLOCK
                    rows = slice(first, first + BLOCK)
                    value = sums[i][0] - sums[i][1 + part]
                    high = value.astype(jnp.bfloat16)
                    low = value - high.astype(jnp.float32)
                    spectra_ref[unit, part, 0, rows] = high
                    spectra_ref[unit, part, 1, rows] = low.astype(jnp.bfloat16)

    def product(table, values):
        return lax.dot_general(
            table, values, (((1,), (1,)), ((), ())), preferred_element_type=jnp.float32
        )

    totals = []
    for part in range(2):
        high, low = (
            jnp.concatenate([spectra_ref[unit, part, half] for unit in range(units)], axis=1)
            for half in range(2)
        )
        tab_high, tab_low = tab_ref[part, 0], tab_ref[part, 1]
        totals.append(product(tab_high, high) + product(tab_low, high) + product(tab_high, low))
    middle = LANES // 2
    chip = lax.axis_index("win") // 2
    low_lanes = lax.broadcasted_iota(jnp.int32, (LAG_ROWS, LANES), 1) < middle
    for core, ref in enumerate((keep_ref, send_ref)):
        even, odd = (total[:LAG_ROWS, core * LANES : (core + 1) * LANES] for total in totals)
        ref[chip] = jnp.where(low_lanes, even, odd)
        ref[1 - chip] = jnp.where(low_lanes, odd, even)


def partial_lags(m, waves, table, after):
    pairs = BLOCK * BLOCK
    planes = pltpu.VMEM((3,) + waves.shape[3:], jnp.float32)
    out = jax.ShapeDtypeStruct((2, LAG_ROWS, LANES), jnp.float32)
    vmem = pl.BlockSpec(memory_space=pltpu.VMEM)
    return pl.pallas_call(
        functools.partial(lag_kernel, m),
        in_specs=[pl.BlockSpec(memory_space=pltpu.SMEM), pl.BlockSpec(memory_space=pl.ANY), vmem],
        out_specs=[vmem, vmem],
        out_shape=[out, out],
        scratch_shapes=[
            pltpu.VMEM(waves.shape[1:], jnp.float32),
            planes,
            pltpu.VMEM((waves.shape[1], 2, 2, pairs, LANES), jnp.bfloat16),
            pltpu.SemaphoreType.DMA(waves.shape[1:2]),
        ],
        compiler_params=pltpu.CompilerParams(vmem_limit_bytes=LAG_VMEM),
        cost_estimate=pl.CostEstimate(flops=4 * 10**9, bytes_accessed=waves.size, transcendentals=0),
        name="partial_lags",
    )(after, waves, table)


def finish_kernel(*refs):
    out_ref = refs[-1]
    total = refs[0][...]
    for ref in refs[1:-1]:
        total = total + ref[...]
    half = LANES // 2
    other = pltpu.roll(total, half, 1)
    low_lanes = lax.broadcasted_iota(jnp.int32, total.shape, 1) < half
    sign = 1.0 - 2.0 * (lax.axis_index("win") // 2).astype(jnp.float32)
    both = jnp.where(low_lanes, sign * (total - other), total + other)
    rows, trailing = out_ref.shape[0], out_ref.shape[1]
    mirror = LANES - 1 - lax.broadcasted_iota(jnp.int32, (half, LANES), 1)
    for k in range(HALF // LANES):
        ahead = both[k * LANES : (k + 1) * LANES, :].T[:half]
        first = HALF + k * LANES
        out_ref[:, :, first : first + LANES] = ahead.reshape(rows, trailing, LANES)
        turned = both[k * LANES + 1 : (k + 1) * LANES + 1, :].T
        behind = jnp.take_along_axis(turned[half:], mirror, axis=1)
        first = HALF - (k + 1) * LANES
        out_ref[:, :, first : first + LANES] = behind.reshape(rows, trailing, LANES)
    last = turned[:half, LANES - 1 :]
    out_ref[:, :, 2 * HALF :] = last.reshape(rows, trailing, 1)


def finish(parts):
    rows = BLOCK // 4
    return pl.pallas_call(
        finish_kernel,
        out_shape=jax.ShapeDtypeStruct((rows, BLOCK, 2 * HALF + 1), jnp.float32),
        name="finish",
    )(*parts)


def by_lags(phases, tile_blocks):
    tile_count = lax.axis_size("tile")
    win_count = lax.axis_size("win")
    windows, bins_local, _ = phases.shape
    tables = jnp.asarray(lag_tables(bins_local * tile_count, bins_local, windows * win_count))
    cross_core = [(w, w ^ 1) for w in range(win_count)]
    cross_chip = [(w, w ^ 2) for w in range(win_count)]
    waves, table = waves_of(phases, tile_blocks, tables, tile_count)
    after = jnp.zeros(1, jnp.int32)
    keep, came, away, part = {}, {}, {}, {}

    def over_core(m):
        keep[m], send = partial_lags(m, waves, table, after)
        came[m] = lax.ppermute(send, "win", cross_core)

    def over_chip(m):
        part[m] = keep[m][0] + came[m][0] + lax.ppermute(away[m], "win", cross_chip)

    def over_tile(m):
        part[m] = lax.ppermute(part[m], "tile", [(z, z ^ m) for z in range(tile_count)])

    over_core(3)
    over_core(2)
    away[3] = keep[3][1] + came[3][1]
    after, away[3] = lax.optimization_barrier((after, away[3]))
    over_chip(3)
    over_core(1)
    away[2] = keep[2][1] + came[2][1]
    after, away[2], part[3] = lax.optimization_barrier((after, away[2], part[3]))
    over_chip(2)
    over_tile(3)
    over_core(0)
    over_tile(2)
    for m in (1, 0):
        away[m] = keep[m][1] + came[m][1]
        over_chip(m)
    over_tile(1)
    parts = [part[m] for m in (3, 2, 1, 0)]
    return finish(parts)[None]


def tables_at(freq_index, bin_count, half_lags, windows):
    freq_index = freq_index[:, None]
    lag_index = jnp.arange(2 * half_lags + 1, dtype=jnp.int32)[None, :] - half_lags
    phase_turns = jnp.mod(freq_index * lag_index, 2 * bin_count).astype(jnp.float32)
    angles = phase_turns * jnp.float32(math.pi / bin_count)
    weight = jnp.where(freq_index == 0, 1.0, 2.0).astype(jnp.float32) / jnp.float32(
        math.sqrt(2.0 * windows * bin_count)
    )
    return (weight * jnp.cos(angles), -weight * jnp.sin(angles))


def cross_spectra(leading, trailing):
    cos_lead, sin_lead = (jnp.cos(leading), jnp.sin(leading))
    cos_trail, sin_trail = (jnp.cos(trailing), jnp.sin(trailing))
    highest = lax.Precision.HIGHEST
    cross_real = jnp.einsum("wfi,wfj->fij", cos_lead, cos_trail, precision=highest) + jnp.einsum(
        "wfi,wfj->fij", sin_lead, sin_trail, precision=highest
    )
    cross_imag = jnp.einsum("wfi,wfj->fij", sin_lead, cos_trail, precision=highest) - jnp.einsum(
        "wfi,wfj->fij", cos_lead, sin_trail, precision=highest
    )
    return (cross_real, cross_imag)


def to_lags(cross_real, cross_imag, cos_tab, sin_tab):
    bin_count, rows_a, rows_b = cross_real.shape
    dims = (((0,), (0,)), ((), ()))
    highest = lax.Precision.HIGHEST
    lagged = lax.dot_general(
        cross_real.reshape(bin_count, rows_a * rows_b), cos_tab, dims, precision=highest
    )
    lagged = lagged + lax.dot_general(
        cross_imag.reshape(bin_count, rows_a * rows_b), sin_tab, dims, precision=highest
    )
    return lagged.reshape(rows_a, rows_b, cos_tab.shape[1])


def by_phases(phases, tile_blocks):
    tile_count = lax.axis_size("tile")
    win_count = lax.axis_size("win")
    win_local = phases.shape[0]
    bins_local = phases.shape[1]
    total_bins = bins_local * tile_count
    total_windows = win_local * win_count
    offsets = jnp.arange(BLOCK, dtype=jnp.int32)
    channels = (tile_blocks[:, :, None] * BLOCK + offsets[None, None, :]).reshape(
        tile_count * 2 * BLOCK
    )
    chosen = jnp.take(phases, channels, axis=2)
    quarter = bins_local // win_count
    received = lax.all_to_all(chosen, "tile", split_axis=2, concat_axis=1, tiled=True)
    shaped = received.reshape(win_local, tile_count, win_count, quarter, 2 * BLOCK)
    arrived = lax.all_to_all(shaped, "win", split_axis=2, concat_axis=0, tiled=True)
    arrived = arrived.reshape(total_windows, tile_count * quarter, 2 * BLOCK)
    source_index = jnp.arange(tile_count, dtype=jnp.int32)[:, None]
    inner_index = jnp.arange(quarter, dtype=jnp.int32)[None, :]
    freq_index = (
        source_index * bins_local + lax.axis_index("win") * quarter + inner_index
    ).reshape(tile_count * quarter)
    cos_tab, sin_tab = tables_at(freq_index, total_bins, HALF, total_windows)
    cross_real, cross_imag = cross_spectra(arrived[:, :, :BLOCK], arrived[:, :, BLOCK:])
    partial_lags = to_lags(cross_real, cross_imag, cos_tab, sin_tab)
    lagged = lax.psum_scatter(partial_lags, "win", scatter_dimension=0, tiled=True)
    return lagged[None]


def on_device(phases, tile_blocks):
    tile_count = lax.axis_size("tile")
    windows, bins_local, _ = phases.shape
    lag_values = tile_count * BLOCK * BLOCK * (2 * HALF + 1)
    phase_values = tile_count * 2 * BLOCK * windows * bins_local
    fits = (
        lax.axis_size("win") == 4
        and tile_count * 2 * BLOCK == LANES
        and bins_local % (4 * LANES) == 0
        and windows % 4 == 0
        and phases.shape[2] % LANES == 0
    )
    if fits and lag_values < phase_values:
        return by_lags(phases, tile_blocks)
    return by_phases(phases, tile_blocks)


def solution(mesh):
    placed = (P(("groups", "win"), "tile", None), P())
    return jax.shard_map(
        on_device,
        mesh=mesh,
        in_specs=placed,
        out_specs=P(("groups", "tile"), "win", None, None),
        check_vma=False,
    )
```
